512 devices in a mesh: tm: 64 (over z, x, core), head: 8 (over y).
Axes of the slice: x: 4, y: 8, z: 8, core: 2. Of those that a mesh axis runs over, the one named last changes fastest.
Arguments:
- query_proj: bfloat16 [8192, 3072], P('tm', 'head'), may hold values from -80 to 80
- key_proj: bfloat16 [8192, 3072], P('tm', 'head'), may hold values from -80 to 80
- value_proj: bfloat16 [8192, 3072], P('tm', 'head'), may hold values from -12 to 12
- query_gain: float32 [3072], P('head'), may hold values from 0.25 to 1.75
- key_gain: float32 [3072], P('head'), may hold values from 0.25 to 1.75
- gate_table: float32 [50, 3072], P(None, 'head'), may hold values from 0.5 to 2
- frame_step: int32 [6], replicated, may hold values from 0 to 49
- far_blocks: int32 [64, 64], P('tm'), may hold values from -1 to 1, as said below
Outputs:
- attended: bfloat16 [8192, 3072], P('tm', 'head')
The draws below stay inside these ranges and needn't reach their ends.
Inputs may be any that keep to these rules, and one draw needn't show every extreme that they name: `far_blocks`: entry [i, j] is the index of the key block of 64 tokens that query block i takes from query block j's tokens, or -1 for none; it is -1 wherever |i - j| <= 1.
All inputs are finite; a program needn't handle non-finite values.
Results may differ from the reference program's by a relative error of at most 0.007.
The reference program's roundings to bfloat16 on the way count: a program that leaves them out, or rounds other values in their place, can miss the bound.
Values may be sent and summed in bfloat16 or wider, within the bound.
A program may use at most 64 MiB of HBM per device.

```python
import jax
import jax.numpy as jnp
from jax import lax

HD = 128
TOK_DEV = 128
BLK = 64
FRAME_TOK = 1560
STEPS = 50
HEADS = 24
TOKENS = 8192
QBLOCKS = 64
FRAMES = 6


def head_rise(ratio):
    return ratio ** (jnp.arange(HEADS, dtype=jnp.float32) / max(HEADS - 1, 1))


def draw_query_proj(key, part):
    key = jax.random.fold_in(key, 11)
    values = jnp.clip(jax.random.normal(key, (TOKENS, HEADS, HD), jnp.float32), -6.0, 6.0) * head_rise(3.0)[None, :, None]
    return values.reshape(TOKENS, HEADS * HD).astype(jnp.bfloat16)


def draw_key_proj(key, part):
    key = jax.random.fold_in(key, 12)
    values = jnp.clip(jax.random.normal(key, (TOKENS, HEADS, HD), jnp.float32), -6.0, 6.0) * head_rise(3.0)[None, :, None]
    return values.reshape(TOKENS, HEADS * HD).astype(jnp.bfloat16)


def draw_far_blocks(key, part):
    key = jax.random.fold_in(key, 7)
    first_key, second_key = jax.random.split(key)
    row_ids = jnp.arange(QBLOCKS, dtype=jnp.int32)[:, None]
    col_ids = jnp.arange(QBLOCKS, dtype=jnp.int32)[None, :]
    distance = jnp.abs(row_ids - col_ids)
    halvings = jnp.minimum(distance * TOK_DEV // (2 * FRAME_TOK), 20)
    threshold = 800 + jnp.right_shift(jnp.full_like(halvings, 200), halvings)
    rolled = jax.random.randint(first_key, (QBLOCKS, QBLOCKS), 0, 1000, dtype=jnp.int32)
    chosen = jax.random.randint(second_key, (QBLOCKS, QBLOCKS), 0, TOK_DEV // BLK, dtype=jnp.int32)
    taken = (rolled < threshold) & (distance > 1)
    return jnp.where(taken, chosen, -1).astype(jnp.int32)


def touch_ends(values, rng, least, largest):
    longest = values.shape.index(max(values.shape))
    spots = []
    for shift in (0, 1):
        where = [jax.random.randint(jax.random.fold_in(rng, axis), (), 0, length) for axis, length in enumerate(values.shape)]
        where[longest] = (where[longest] + shift) % values.shape[longest]
        spots.append(tuple(where))
    return values.at[spots[0]].set(least).at[spots[1]].set(largest)


def steps_of(stream_key, extent, cuts, smallest, largest):
    level, own = 1.0, jax.random.fold_in(stream_key, 6)
    for dim, shards_of in cuts:
        steps = jnp.exp(jax.random.uniform(jax.random.fold_in(own, dim), (shards_of,), jnp.float32, smallest / len(cuts), largest / len(cuts)))
        level = level * jnp.repeat(steps, extent[dim] // shards_of).reshape([-1 if axis == dim else 1 for axis in range(len(extent))])
    return level


def bell_draw(stream_key, shape, deviation, reach, shards=(), held_as=jnp.bfloat16):
    drawn = deviation * jax.random.normal(stream_key, shape, jnp.float32)
    if shards:
        drawn = drawn * steps_of(stream_key, shape, shards, -0.22, 0.18)
    return jnp.clip(drawn, -reach, reach).astype(held_as)


def setup_inputs(seed: int = 0) -> dict:
    key_list = jax.random.split(jax.random.key(seed), 9)
    query_proj = draw_query_proj(jax.random.fold_in(key_list[8], 71), 0)
    key_proj = draw_key_proj(jax.random.fold_in(key_list[8], 71), 0)
    value_proj = bell_draw(key_list[2], (TOKENS, HEADS * HD), 2.0, 12.0, ((0, 64), (1, 8)))
    query_gain = jnp.clip(1.0 + 0.15 * jax.random.normal(key_list[3], (HEADS * HD,), jnp.float32), 0.25, 1.75)
    key_gain = jnp.clip(1.0 + 0.15 * jax.random.normal(key_list[4], (HEADS * HD,), jnp.float32), 0.25, 1.75)
    gate_table = jnp.clip(0.5 + 1.5 * jax.random.uniform(key_list[5], (STEPS, HEADS * HD), jnp.float32) ** steps_of(key_list[5], (STEPS, HEADS * HD), ((1, 8),), -0.2, 0.2), 0.5, 2.0)
    frame_step = touch_ends(jax.random.randint(key_list[6], (FRAMES,), 0, STEPS), jax.random.fold_in(key_list[6], 1), 0, STEPS - 1).astype(jnp.int32)
    far_blocks = draw_far_blocks(jax.random.fold_in(key_list[8], 71), 0)
    return {"query_proj": query_proj, "key_proj": key_proj, "value_proj": value_proj, "query_gain": query_gain, "key_gain": key_gain, "gate_table": gate_table, "frame_step": frame_step, "far_blocks": far_blocks}


def normed(source, gain):
    source_f = source.astype(jnp.float32)
    mean_sq = lax.optimization_barrier(jnp.mean(source_f * source_f, axis=-1, keepdims=True))
    return (source_f * lax.rsqrt(mean_sq + 1e-06) * gain).astype(jnp.bfloat16)

def reference(query_proj, key_proj, value_proj, query_gain, key_gain, gate_table, frame_step, far_blocks):
    feat_width = HEADS * HD
    block_count = TOK_DEV // BLK
    query_norm = normed(query_proj, query_gain)
    key_norm = normed(key_proj, key_gain)
    padded_keys = jnp.pad(key_norm, ((TOK_DEV, TOK_DEV), (0, 0)))
    padded_values = jnp.pad(value_proj, ((TOK_DEV, TOK_DEV), (0, 0)))
    key_blocks = key_norm.reshape(QBLOCKS, block_count, BLK, feat_width)
    value_blocks = value_proj.reshape(QBLOCKS, block_count, BLK, feat_width)
    segment = jnp.arange(3 * TOK_DEV, dtype=jnp.int32) // TOK_DEV
    owners = jnp.arange(QBLOCKS, dtype=jnp.int32)
    score_scale = HD ** (-0.5)

    def one_block(block_id):
        start = (block_id * TOK_DEV).astype(jnp.int32)
        query_rows = lax.dynamic_slice_in_dim(query_norm, start, TOK_DEV, 0)
        band_keys = lax.dynamic_slice_in_dim(padded_keys, start, 3 * TOK_DEV, 0)
        band_values = lax.dynamic_slice_in_dim(padded_values, start, 3 * TOK_DEV, 0)
        band_mask = (segment == 1) | (segment == 0) & (block_id > 0) | (segment == 2) & (block_id < QBLOCKS - 1)
        chosen = far_blocks[block_id]
        picked = jnp.maximum(chosen, 0).astype(jnp.int32)
        far_keys = key_blocks[owners, picked].reshape(QBLOCKS * BLK, feat_width)
        far_values = value_blocks[owners, picked].reshape(QBLOCKS * BLK, feat_width)
        far_mask = jnp.repeat(chosen >= 0, BLK)
        all_keys = jnp.concatenate([band_keys, far_keys], axis=0)
        all_values = jnp.concatenate([band_values, far_values], axis=0)
        key_mask = jnp.concatenate([band_mask, far_mask], axis=0)
        query_heads = query_rows.astype(jnp.float32).reshape(TOK_DEV, HEADS, HD)
        key_heads = all_keys.astype(jnp.float32).reshape(-1, HEADS, HD)
        value_heads = all_values.astype(jnp.float32).reshape(-1, HEADS, HD)
        scores = jnp.einsum('qhd,khd->hqk', query_heads, key_heads) * score_scale
        scores = jnp.where(key_mask[None, None, :], scores, -jnp.inf)
        row_max = lax.optimization_barrier(jnp.max(scores, axis=-1, keepdims=True))
        weights = jnp.exp(scores - row_max)
        totals = lax.optimization_barrier(jnp.sum(weights, axis=-1))
        rounded = weights.astype(jnp.bfloat16).astype(jnp.float32)
        context = jnp.einsum('hqk,khd->qhd', rounded, value_heads) / jnp.transpose(totals)[:, :, None]
        positions = start + jnp.arange(TOK_DEV, dtype=jnp.int32)
        steps_here = frame_step[positions // FRAME_TOK]
        gate = gate_table[steps_here]
        return (context.reshape(TOK_DEV, feat_width) * gate).astype(jnp.bfloat16)
    result = lax.map(one_block, jnp.arange(QBLOCKS, dtype=jnp.int32))
    return result.reshape(TOKENS, feat_width)
```

```python
import functools

import jax
import jax.numpy as jnp
from jax import lax
from jax.experimental import pallas as pl
from jax.experimental.pallas import tpu as pltpu
from jax.sharding import PartitionSpec as P

HD = 128
TOK = 128
BLK = 64
FRAME_TOK = 1560
NZ, NX, NC = 8, 4, 2
NH = 3
EPS = 1e-06
MASKED = -1e30
GROUP = 4
LOG2E = 1.4426950408889634
COEF = HD**-0.5 * LOG2E
MESH = pl.DeviceIdType.MESH
BF16 = jnp.bfloat16
F32 = jnp.float32


def kernel(
    ny,
    q_hbm, k_hbm, v_hbm, qg_hbm, kg_hbm, gate_hbm, frame_ref, far_ref,
    out_ref,
    qin, kin, qg_in, kg_in, gate_in, qst,
    v_own, v_left, v_right, v_far, k_own, k_left, k_right, k_far, k_raw, isc, inv_buf, qbuf, fst, fbuf, fsm, sst, sbuf, bias,
    m_ref, l_ref, acc_ref, ost, stst, obuf, stb,
    load_sem, own_sem, fsm_sem,
    s_send, s_recv, f_send, f_recv, q_send, q_recv,
    p1_send, p1_recv, i_send, i_recv, x_send, x_recv, c_send, c_recv,
    o_send, o_recv, t_send, t_recv,
):
    tm = lax.axis_index("tm")
    y = lax.axis_index("head")
    c = lax.rem(tm, NC)
    x = lax.rem(tm // NC, NX)
    z = tm // (NC * NX)
    head = lax.rem(z, 4)
    active = head < NH
    xl, xr = lax.rem(x + 3, NX), lax.rem(x + 1, NX)
    colx = (x, xl, xr, lax.rem(x + 2, NX))

    def dev(zz, xx, cc):
        return (zz * (NX * NC) + xx * NC + cc, y)

    def remote(src, dst, ss, rs, target):
        return pltpu.make_async_remote_copy(
            src_ref=src, dst_ref=dst, send_sem=ss, recv_sem=rs,
            device_id=target, device_id_type=MESH,
        )

    loads = [
        pltpu.make_async_copy(s, d, load_sem.at[i])
        for i, (s, d) in enumerate(((k_hbm, kin), (q_hbm, qin)))
    ]
    late_loads = [
        pltpu.make_async_copy(s, d, load_sem.at[2 + i])
        for i, (s, d) in enumerate(((qg_hbm, qg_in), (kg_hbm, kg_in), (gate_hbm, gate_in)))
    ]
    for cp in loads + late_loads:
        cp.start()

    barrier = pltpu.get_barrier_semaphore()
    partners = [(tm, lax.rem(y + d, ny)) for d in range(1, ny)]
    partners += [dev(lax.rem(z + d, NZ), x, c) for d in range(1, NZ)]
    partners += [dev(z, xl, c), dev(z, xr, c), dev(z, x, 1 - c)]
    for p in partners:
        pl.semaphore_signal(barrier, inc=1, device_id=p, device_id_type=MESH)

    for cp in loads:
        cp.wait()

    def square_sums(ref):
        f = ref[...].astype(F32)
        sq = f * f
        part = sq[:, 0:HD] + sq[:, HD : 2 * HD] + sq[:, 2 * HD : 3 * HD]
        return jnp.sum(part.T, axis=0, keepdims=True)

    sst[...] = jnp.concatenate(
        [square_sums(qin), square_sums(kin), jnp.zeros((6, TOK), F32)], axis=0
    )
    sbuf[y] = sst[...]
    far_row = jnp.concatenate([far_ref[...], jnp.full((1, 64), -1, jnp.int32)], axis=1)
    fst[...] = jnp.broadcast_to(far_row, (8, 128))

    pl.semaphore_wait(barrier, len(partners))

    s_copies = []
    for d in range(1, ny):
        cp = remote(sst, sbuf.at[y], s_send.at[d - 1], s_recv.at[d - 1], (tm, lax.rem(y + d, ny)))
        cp.start()
        s_copies.append(cp)

    place = []
    for h in range(NH):
        k = lax.rem(z - h + 1 + NZ, NZ)
        place.append((h + 4 * (k // 4), lax.rem(k, 4)))

    def row_copies(t, h):
        row, slot = place[h]
        cols = pl.ds(h * HD, HD)
        if t == 1:
            ends = [(k_hbm.at[:, cols], k_raw.at[slot])]
        else:
            ends = [(v_hbm.at[pl.ds(p * BLK, BLK), cols], v_own.at[c, slot, p]) for p in range(2)]
        return [
            remote(src, dst, p1_send.at[t + p, h], p1_recv.at[t, slot], dev(row, x, c))
            for p, (src, dst) in zip((0, 2), ends)
        ]

    def inv_copy(h):
        row, slot = place[h]
        return remote(isc, inv_buf.at[slot], i_send.at[h], i_recv.at[slot], dev(row, x, c))

    def own_copies(t, h):
        cols = pl.ds(h * HD, HD)
        if t == 1:
            return [pltpu.make_async_copy(k_hbm.at[:, cols], k_raw.at[1], own_sem.at[2])]
        return [
            pltpu.make_async_copy(
                v_hbm.at[pl.ds(p * BLK, BLK), cols], v_own.at[c, 1, p], own_sem.at[p]
            )
            for p in range(2)
        ]

    def to_rows(t):
        for h, (row, _) in enumerate(place):

            @pl.when(row != z)
            def _():
                for cp in row_copies(t, h):
                    cp.start()

            @pl.when(row == z)
            def _():
                for cp in own_copies(t, h):
                    cp.start()

    def row_arrived(t, slot):
        if slot == 1:
            for cp in own_copies(t, 0):
                cp.wait()
        else:
            ref = k_raw.at[slot] if t == 1 else v_own.at[c, slot]
            remote(
                ref, ref, p1_send.at[t, 0], p1_recv.at[t, slot], dev(z, x, 1 - c)
            ).wait_recv()

    bufs = ((v_own, v_left, v_right, v_far), (k_own, k_left, k_right, k_far))

    def x_copy(t, lane, item):
        if item < 2:
            here, there, half = 0, 1 + lane, item
        else:
            here, there, half = 1 + lane, 3, lane
        part = pl.ds(2 * half, 2)
        return remote(
            bufs[t][here].at[c, part], bufs[t][there].at[c, part],
            x_send.at[t, lane, item], x_recv.at[t, lane, item],
            dev(z, xr if lane == 0 else xl, c),
        )

    def x_arrived(t, lane, item):
        x_copy(t, lane, item).wait_recv()

    def c_copy(t, col, half):
        ref = bufs[t][col].at[c, pl.ds(2 * half, 2)]
        return remote(
            ref, ref, c_send.at[t, col, half], c_recv.at[t, col, half], dev(z, x, 1 - c)
        )

    def c_arrived(t, col):
        for half in range(2):
            ref = bufs[t][col].at[1 - c, pl.ds(2 * half, 2)]
            remote(
                ref, ref, c_send.at[t, col, half], c_recv.at[t, col, half], dev(z, x, 1 - c)
            ).wait_recv()

    def key_ready(slot):
        row_arrived(1, slot)
        if slot != 1:
            remote(
                isc, inv_buf.at[slot], i_send.at[0], i_recv.at[slot], dev(z, x, 1 - c)
            ).wait_recv()
        scale = jnp.broadcast_to(inv_buf[slot][1:2, :], (TOK, HD)).T
        gain = kg_in[pl.ds(pl.multiple_of(head * HD, HD), HD)].reshape(1, HD)
        keys = (k_raw[slot].astype(F32) * scale * gain).astype(BF16)
        k_own[c, slot] = keys.reshape(2, BLK, HD)

    def spread_own(t):
        ready = key_ready if t == 1 else functools.partial(row_arrived, 0)
        ready(1)
        ready(0)
        x_copy(t, 0, 0).start()
        c_copy(t, 0, 0).start()
        ready(2)
        ready(3)
        x_copy(t, 1, 1).start()
        x_copy(t, 0, 1).start()
        x_copy(t, 1, 0).start()
        c_copy(t, 0, 1).start()

    def relay(t):
        x_arrived(t, 0, 0)
        x_copy(t, 0, 2).start()
        c_copy(t, 1, 0).start()
        x_arrived(t, 1, 1)
        x_copy(t, 1, 2).start()
        c_copy(t, 2, 1).start()

    def rest(t):
        x_arrived(t, 0, 1)
        c_copy(t, 1, 1).start()
        x_arrived(t, 1, 0)
        c_copy(t, 2, 0).start()

    def opposite(t):
        x_arrived(t, 0, 2)
        c_copy(t, 3, 0).start()
        x_arrived(t, 1, 2)
        c_copy(t, 3, 1).start()

    to_rows(0)
    to_rows(1)

    rows = [(h, part) for h in range(NH) for part in range(2)]

    def f_copy(i):
        h, part = rows[i]
        return remote(fst, fbuf.at[z], f_send.at[i], f_recv.at[z], dev(h + 4 * part, x, c))

    def q_copy(i):
        h, part = rows[i]
        return remote(qst.at[h], qbuf.at[z], q_send.at[i], q_recv.at[z], dev(h + 4 * part, x, c))

    for i, (h, part) in enumerate(rows):

        @pl.when(h + 4 * part != z)
        def _():
            f_copy(i).start()

    fbuf[z] = fst[...]

    @pl.when(active)
    def _():
        spread_own(0)

    for cp in s_copies:
        cp.wait()
    totals = sbuf[0]
    for i in range(1, ny):
        totals = totals + sbuf[i]
    for cp in late_loads:
        cp.wait()
    inv = lax.rsqrt(totals / (NH * HD * ny) + EPS)

    def normed(ref, row, gain_ref, h):
        span = slice(h * HD, (h + 1) * HD)
        scale = jnp.broadcast_to(inv[row : row + 1, :], (TOK, HD)).T
        return (ref[:, span].astype(F32) * scale * gain_ref[span].reshape(1, HD)).astype(BF16)

    isc[...] = inv
    inv_buf[1] = inv
    for h, (row, _) in enumerate(place):

        @pl.when(row != z)
        def _():
            inv_copy(h).start()

    for h in range(NH):
        qst[h] = normed(qin, 0, qg_in, h)
    for i, (h, part) in enumerate(rows):

        @pl.when(h + 4 * part != z)
        def _():
            q_copy(i).start()

        @pl.when(h + 4 * part == z)
        def _():
            qbuf[z] = qst[h]

    lane = lax.broadcasted_iota(jnp.int32, (1, HD), 1)
    lane_sq = lax.broadcasted_iota(jnp.int32, (TOK, HD), 1)

    def o_copy(zz):
        return remote(
            ost.at[zz], obuf.at[head, z // 4], o_send.at[zz], o_recv.at[head, z // 4], dev(zz, x, c)
        )

    def t_copy(zz):
        return remote(
            stst.at[zz], stb.at[head, z // 4], t_send.at[zz], t_recv.at[head, z // 4], dev(zz, x, c)
        )

    def band_slot(zz, d):
        j = zz * 8 + x * 2 + c + d
        zj = jnp.clip(j, 0, 63) // 8
        slot = lax.rem(zj - z + 1 + NZ, NZ)
        ok = (slot < 4) & (j >= 0) & (j <= 63)
        return jnp.minimum(slot, 3), jnp.where(ok, 0.0, MASKED).astype(F32)

    def half(ref, core, slot, pick):
        return ref[core, slot, pick]

    def attend(col, zz):
        key_parts, value_parts = [], []
        keys_of, values_of = bufs[1][col], bufs[0][col]
        for core in range(NC):
            for slot in range(4):
                owner = lax.rem(z - 1 + slot + NZ, NZ) * 8 + colx[col] * 2 + core
                pick = jnp.maximum(fsm[zz, 0, owner], 0)
                key_parts.append(half(keys_of, core, slot, pick))
                value_parts.append(half(values_of, core, slot, pick))
        add = [bias[col, pl.ds(zz, 1), :]]
        if col == 0:
            slot, own = band_slot(zz, 0)
            slot_two, two = band_slot(zz, 1 - 2 * c)
            for core, at in ((c, slot), (1 - c, slot_two)):
                key_parts.append(half(keys_of, core, at, 1))
                value_parts.append(half(values_of, core, at, 1))
            add.append(jnp.where(lane < BLK, own, two))
        if col == 3:
            slot, ok = band_slot(zz, 2 * c - 1)
            for of, parts in ((bufs[1], key_parts), (bufs[0], value_parts)):
                part = jnp.where(c == 0, half(of[1], 1, slot, 1), half(of[2], 0, slot, 1))
                parts += [part, part]
            add.append(jnp.where(lane < BLK, ok, MASKED))
        keys = jnp.concatenate(key_parts, axis=0)
        values = jnp.concatenate(value_parts, axis=0)
        scores = lax.dot_general(
            qbuf[zz], keys, (((1,), (1,)), ((), ())), preferred_element_type=F32
        ) + jnp.concatenate(add, axis=1)
        return [scores[:, i * HD : (i + 1) * HD] for i in range(scores.shape[1] // HD)], values

    def chunk_steps(col, blocks):
        first, last = col == 0, col == 3
        scored = [attend(col, zz) for zz in blocks]
        tops, fades, totals_of, contexts = [], [], [], []
        for zz, (tiles, _) in zip(blocks, scored):
            top = functools.reduce(jnp.maximum, tiles)
            top = jnp.broadcast_to(jnp.max(top, axis=1, keepdims=True), (TOK, HD))
            if not first:
                old = m_ref[zz]
                top = jnp.maximum(old, top)
                fades.append(jnp.exp2((old - top) * COEF))
            tops.append(top)
        for i, (zz, (tiles, values)) in enumerate(zip(blocks, scored)):
            tiles = [jnp.exp2((t - tops[i]) * COEF) for t in tiles]
            total = functools.reduce(jnp.add, tiles)
            weights = jnp.concatenate([t.astype(BF16) for t in tiles], axis=1)
            context = jnp.dot(weights, values, preferred_element_type=F32)
            if not first:
                total = l_ref[zz] * fades[i] + total
                context = acc_ref[zz] * fades[i] + context
            totals_of.append(total)
            contexts.append(context)
        if not last:
            for zz, top, total, context in zip(blocks, tops, totals_of, contexts):
                m_ref[zz] = top
                l_ref[zz] = total
                acc_ref[zz] = context
            return
        results = []
        for top, total, context in zip(tops, totals_of, contexts):
            total = jnp.broadcast_to(jnp.sum(total, axis=1, keepdims=True), (TOK, HD))
            stats = jnp.where(lane_sq == 0, top, total).T[0:8]
            results.append(((context / total).astype(BF16), stats))
        for zz, (context, stats) in zip(blocks, results):
            ost[zz] = context
            stst[zz] = stats
        for zz, (context, stats) in zip(blocks, results):

            @pl.when(zz == z)
            def _():
                obuf[head, z // 4] = context
                stb[head, z // 4] = stats

            @pl.when(zz != z)
            def _():
                o_copy(zz).start()
                t_copy(zz).start()

    def chunk(col):
        def body(i, carry):
            blocks = []
            for j in range(GROUP):
                k = (GROUP // 2) * i + (j + 1) // 2
                blocks.append(lax.rem(z + 4 + (k if j % 2 == 0 else -k) + NZ, NZ))
            chunk_steps(col, blocks)
            return carry

        lax.fori_loop(0, NZ // GROUP, body, 0)

    @pl.when(active)
    def _():
        for d in range(1, NZ):
            zz = lax.rem(z + d, NZ)
            remote(fst, fbuf.at[zz], f_send.at[0], f_recv.at[zz], dev(zz, x, c)).wait_recv()
        cp = pltpu.make_async_copy(fbuf, fsm, fsm_sem)
        cp.start()
        relay(0)
        spread_own(1)
        far = fbuf[:, 0, 0:64]
        block = lax.broadcasted_iota(jnp.int32, (NZ, 64), 0) * 8 + x * 2 + c
        other = lax.broadcasted_iota(jnp.int32, (NZ, 64), 1)
        valid = jnp.where((far >= 0) | (jnp.abs(block - other) <= 1), 1.0, 0.0).astype(BF16)
        at = lax.broadcasted_iota(jnp.int32, (64, 512), 1) // BLK
        src = lax.broadcasted_iota(jnp.int32, (64, 512), 0)
        zsrc = lax.rem(z - 1 + lax.rem(at, 4) + NZ, NZ)
        for col in range(NX):
            spread = (src == zsrc * 8 + colx[col] * 2 + at // 4).astype(F32).astype(BF16)
            hit = jnp.dot(valid, spread, preferred_element_type=F32)
            bias[col] = jnp.where(hit > 0.5, 0.0, MASKED)
        rest(0)
        opposite(0)
        cp.wait()
        relay(1)
        for d in range(1, NZ):
            zz = lax.rem(z + d, NZ)
            remote(qst.at[0], qbuf.at[zz], q_send.at[0], q_recv.at[zz], dev(zz, x, c)).wait_recv()
        c_arrived(0, 0)
        c_arrived(1, 0)
        chunk(0)
        rest(1)
        c_arrived(0, 1)
        c_arrived(1, 1)
        chunk(1)
        opposite(1)
        c_arrived(0, 2)
        c_arrived(1, 2)
        chunk(2)
        c_arrived(0, 3)
        c_arrived(1, 3)
        chunk(3)

    start = tm * TOK
    frame = start // FRAME_TOK
    after = jnp.minimum(frame + 1, 5)
    steps = lax.broadcasted_iota(jnp.int32, gate_in.shape, 0)

    def gate_of(step):
        return jnp.sum(jnp.where(steps == step, gate_in[...], 0.0), axis=0, keepdims=True)

    gate_a, gate_b = gate_of(frame_ref[frame]), gate_of(frame_ref[after])
    edge = (frame + 1) * FRAME_TOK - start
    before = lax.broadcasted_iota(jnp.int32, (TOK, HD), 0) < edge
    for h in range(NH):
        for part in range(2):

            @pl.when(h + 4 * part != z)
            def _():
                remote(
                    ost.at[0], obuf.at[h, part], o_send.at[0], o_recv.at[h, part], dev(z, x, 1 - c)
                ).wait_recv()
                remote(
                    stst.at[0], stb.at[h, part], t_send.at[0], t_recv.at[h, part], dev(z, x, 1 - c)
                ).wait_recv()

        span = slice(h * HD, (h + 1) * HD)
        one, two = stb[h, 0], stb[h, 1]
        top = jnp.maximum(one[0:1], two[0:1])
        weight_one = one[1:2] * jnp.exp2((one[0:1] - top) * COEF)
        weight_two = two[1:2] * jnp.exp2((two[0:1] - top) * COEF)
        share = weight_one / (weight_one + weight_two)
        share = jnp.broadcast_to(share, (TOK, HD)).T
        context = obuf[h, 0].astype(F32) * share + obuf[h, 1].astype(F32) * (1.0 - share)
        gate = jnp.where(before, gate_a[:, span], gate_b[:, span])
        out_ref[:, span] = (context * gate).astype(BF16)

    for h, (row, _) in enumerate(place):

        @pl.when(row != z)
        def _():
            for cp in row_copies(0, h) + row_copies(1, h):
                cp.wait_send()
            inv_copy(h).wait_send()

    for i, (h, part) in enumerate(rows):

        @pl.when(h + 4 * part != z)
        def _():
            f_copy(i).wait_send()
            q_copy(i).wait_send()

    @pl.when(active)
    def _():
        for t in range(2):
            for ln in range(2):
                for item in range(3):
                    x_copy(t, ln, item).wait_send()
            for col in range(4):
                for half in range(2):
                    c_copy(t, col, half).wait_send()
        for d in range(1, NZ):
            zz = lax.rem(z + d, NZ)
            o_copy(zz).wait_send()
            t_copy(zz).wait_send()


def solution(mesh):
    ny = mesh.shape["head"]
    dma = pltpu.SemaphoreType.DMA
    vmem = pltpu.VMEM

    def local(query, key, value, query_gain, key_gain, gate_table, frame_step, far_blocks):
        whole = pl.BlockSpec(memory_space=pltpu.VMEM)
        hbm = pl.BlockSpec(memory_space=pltpu.HBM)
        width = NH * HD
        return pl.pallas_call(
            functools.partial(kernel, ny),
            out_shape=jax.ShapeDtypeStruct((TOK, width), BF16),
            in_specs=[hbm] * 6 + [pl.BlockSpec(memory_space=pltpu.SMEM), whole],
            out_specs=whole,
            scratch_shapes=[
                vmem((TOK, width), BF16),
                vmem((TOK, width), BF16),
                vmem((width,), F32),
                vmem((width,), F32),
                vmem((50, width), F32),
                vmem((NH, TOK, HD), BF16),
                *[vmem((NC, 4, 2, BLK, HD), BF16)] * 8,
                vmem((4, TOK, HD), BF16),
                vmem((8, TOK), F32),
                vmem((4, 8, TOK), F32),
                vmem((NZ, TOK, HD), BF16),
                vmem((8, 128), jnp.int32),
                vmem((NZ, 8, 128), jnp.int32),
                pltpu.SMEM((NZ, 8, 128), jnp.int32),
                vmem((8, TOK), F32),
                vmem((ny, 8, TOK), F32),
                vmem((NX, NZ, 512), F32),
                vmem((NZ, TOK, HD), F32),
                vmem((NZ, TOK, HD), F32),
                vmem((NZ, TOK, HD), F32),
                vmem((NZ, TOK, HD), BF16),
                vmem((NZ, 8, TOK), F32),
                vmem((NH, 2, TOK, HD), BF16),
                vmem((NH, 2, 8, TOK), F32),
                dma((5,)), dma((3,)), dma,
                dma((ny,)), dma((ny,)), dma((6,)), dma((NZ,)), dma((6,)), dma((NZ,)),
                dma((3, 3)), dma((2, 4)), dma((3,)), dma((4,)), dma((2, 2, 3)), dma((2, 2, 3)),
                dma((2, 4, 2)), dma((2, 4, 2)),
                dma((NZ,)), dma((NH, 2)), dma((NZ,)), dma((NH, 2)),
            ],
            compiler_params=pltpu.CompilerParams(
                collective_id=0, has_side_effects=True, vmem_limit_bytes=56 * 2**20
            ),
            name="attend",
        )(
            query, key, value, query_gain, key_gain,
            gate_table, frame_step, far_blocks,
        )

    return jax.shard_map(
        local,
        mesh=mesh,
        in_specs=(
            P("tm", "head"),
            P("tm", "head"),
            P("tm", "head"),
            P("head"),
            P("head"),
            P(None, "head"),
            P(),
            P("tm", None),
        ),
        out_specs=P("tm", "head"),
        check_vma=False,
    )
```

```python
import functools

import jax
import jax.numpy as jnp
from jax import lax
from jax.experimental import pallas as pl
from jax.experimental.pallas import tpu as pltpu
from jax.sharding import PartitionSpec as P

HD = 128
TOK = 128
BLK = 64
FRAME_TOK = 1560
NZ, NX, NC = 8, 4, 2
NH = 3
EPS = 1e-06
MASKED = -1e30
GROUP = 4
LOG2E = 1.4426950408889634
COEF = HD**-0.5 * LOG2E
MESH = pl.DeviceIdType.MESH
BF16 = jnp.bfloat16
F32 = jnp.float32

ROWS = (0, 1, 2, 4, 5, 6)


def kernel(
    ny,
    q_hbm, k_hbm, v_hbm, qg_hbm, kg_hbm, gate_hbm, frame_ref, far_ref,
    out_ref,
    qin, kin, qg_in, kg_in, gate_in, q_raw, k_raw, v_raw, isc, inv_own, inv_buf, qbuf,
    fst, fbuf, fsm, sst, sbuf, bias, m_ref, l_ref, acc_ref, ost, stst, obuf, stb,
    *rest,
):
    keys_at, values_at = (rest[0:4], rest[4:8]), (rest[8:12], rest[12:16])
    (
        load_sem, own_sem, fsm_sem, hello, hello_y,
        s_send, s_recv, f_send, f_recv, q_send, q_recv,
        p1_send, p1_recv, io_send, io_recv, i_send, i_recv, x_send, x_recv, c_send, c_recv,
        o_send, o_recv, t_send, t_recv,
    ) = rest[16:]
    tm = lax.axis_index("tm")
    y = lax.axis_index("head")
    c = lax.rem(tm, NC)
    x = lax.rem(tm // NC, NX)
    z = tm // (NC * NX)
    part, slot_mine = z // 4, lax.rem(z, 4)
    active = slot_mine < 3
    head = jnp.minimum(slot_mine, 2)
    xl, xr = lax.rem(x + 3, NX), lax.rem(x + 1, NX)
    colx = (x, xl, xr, lax.rem(x + 2, NX))

    def dev(zz, xx, cc):
        return (zz * (NX * NC) + xx * NC + cc, y)

    def remote(src, dst, ss, rs, target):
        return pltpu.make_async_remote_copy(
            src_ref=src, dst_ref=dst, send_sem=ss, recv_sem=rs,
            device_id=target, device_id_type=MESH,
        )

    loads = [
        pltpu.make_async_copy(s, d, load_sem.at[i])
        for i, (s, d) in enumerate(((k_hbm, kin), (q_hbm, qin)))
    ]
    late_loads = [
        pltpu.make_async_copy(s, d, load_sem.at[2 + i])
        for i, (s, d) in enumerate(((qg_hbm, qg_in), (kg_hbm, kg_in), (gate_hbm, gate_in)))
    ]
    for cp in loads + late_loads:
        cp.start()

    barrier = pltpu.get_barrier_semaphore()

    def greet(target):
        pl.semaphore_signal(barrier, inc=1, device_id=target, device_id_type=MESH)

    for d in range(1, NX):
        greet(dev(z, lax.rem(x + d, NX), c))
    greet(dev(z, x, 1 - c))
    for yy in range(1, ny):

        @pl.when(yy > y)
        def _():
            greet((tm, yy))

    for zz in range(1, NZ):

        @pl.when(zz > z)
        def _():
            greet(dev(zz, x, c))

        @pl.when((zz > z) & (zz // 4 == part))
        def _():
            for d in range(1, NX):
                greet(dev(zz, lax.rem(x + d, NX), c))

    pl.semaphore_wait(barrier, NX + z + 3 * slot_mine + y)

    for zz in range(NZ - 1):

        @pl.when(active & (zz < z))
        def _():
            pl.semaphore_signal(hello.at[z], inc=1, device_id=dev(zz, x, c), device_id_type=MESH)

    for yy in range(ny - 1):

        @pl.when(yy < y)
        def _():
            pl.semaphore_signal(hello_y.at[y], inc=1, device_id=(tm, yy), device_id_type=MESH)

    def await_row(row):
        @pl.when(row > z)
        def _():
            pl.semaphore_wait(hello.at[row], 1)

    def row_copies(h):
        row, cols = h + 4 * part, pl.ds(h * HD, HD)
        return [
            remote(
                ref.at[:, cols], dst, p1_send.at[t, h], p1_recv.at[t, slot_mine], dev(row, x, c)
            )
            for t, (ref, dst) in enumerate(
                ((v_hbm, v_raw.at[slot_mine]), (k_hbm, k_raw.at[0, slot_mine]))
            )
        ]

    def own_copy(t, h):
        ref, dst = (
            (v_hbm, v_raw.at[slot_mine]), (k_hbm, k_raw.at[0, slot_mine]), (q_hbm, q_raw.at[z])
        )[t]
        return pltpu.make_async_copy(ref.at[:, pl.ds(h * HD, HD)], dst, own_sem.at[t])

    def f_copy(i):
        return remote(fst, fbuf.at[z], f_send.at[i], f_recv.at[z], dev(ROWS[i], x, c))

    def q_copy(i):
        source = q_hbm.at[:, pl.ds(i % NH * HD, HD)]
        return remote(source, q_raw.at[z], q_send.at[i], q_recv.at[z], dev(ROWS[i], x, c))

    def queries_to(i):
        @pl.when(ROWS[i] != z)
        def _():
            f_copy(i).start()
            q_copy(i).start()

    far_row = jnp.concatenate([far_ref[...], jnp.full((1, 64), -1, jnp.int32)], axis=1)
    fst[...] = jnp.broadcast_to(far_row, (8, 128))
    fbuf[z] = fst[...]
    for p in range(2):

        @pl.when(part == p)
        def _():
            for h in range(NH):
                row = h + 4 * p
                await_row(row)

                @pl.when(row != z)
                def _():
                    for cp in row_copies(h):
                        cp.start()

                @pl.when(row == z)
                def _():
                    for t in range(3):
                        own_copy(t, h).start()

    for cp in loads:
        cp.wait()

    def square_sums(ref):
        f = ref[...].astype(F32)
        sq = f * f
        sq = sq[:, 0:HD] + sq[:, HD : 2 * HD] + sq[:, 2 * HD : 3 * HD]
        return jnp.sum(sq.T, axis=0, keepdims=True)

    sst[...] = jnp.concatenate(
        [square_sums(qin), square_sums(kin), jnp.zeros((6, TOK), F32)], axis=0
    )
    sbuf[y] = sst[...]

    def s_copy(yy):
        return remote(sst, sbuf.at[y], s_send.at[yy], s_recv.at[y], (tm, yy))

    for yy in range(ny - 1):

        @pl.when(yy < y)
        def _():
            s_copy(yy).start()

    @pl.when(part == 0)
    def _():
        for i in range(3):
            queries_to(i)

    for yy in range(1, ny):

        @pl.when(yy > y)
        def _():
            pl.semaphore_wait(hello_y.at[yy], 1)
            s_copy(yy).start()

    def arrived(ref, sem):
        remote(ref, ref, s_send.at[0], sem, dev(z, x, 1 - c)).wait_recv()

    def row_arrived(t, slot):
        ref = (v_raw.at[slot], k_raw.at[0, slot])[t]

        @pl.when(slot == slot_mine)
        def _():
            own_copy(t, 0).wait()

        @pl.when(slot != slot_mine)
        def _():
            arrived(ref, p1_recv.at[t, slot])

    def k_half(col, half):
        return k_raw.at[col, pl.ds(2 * half, 2)]

    def x_copy(t, lane, half):
        if t == 1:
            src, dst = k_half(0, half), k_half(1 + lane, half)
        else:
            src, dst = values_at[half][0].at[c], values_at[half][1 + lane].at[c]
        return remote(
            src, dst, x_send.at[t, lane, half], x_recv.at[t, lane, half],
            dev(z, lax.rem(x + (1, 3, 2)[lane], NX), c),
        )

    def x_arrived(t, lane, half):
        x_copy(t, lane, half).wait_recv()

    def c_copy(t, col, half):
        ref = (values_at, keys_at)[t][half][col].at[c]
        return remote(
            ref, ref, c_send.at[t, col, half], c_recv.at[t, col, half], dev(z, x, 1 - c)
        )

    def c_arrived(t, col, half):
        arrived((values_at, keys_at)[t][half][col].at[1 - c], c_recv.at[t, col, half])

    def spread_own(half):
        for slot in (2 * half, 2 * half + 1):
            row_arrived(1, slot)
        for ln in (2, 0, 1):
            x_copy(1, ln, half).start()
        for slot in (2 * half, 2 * half + 1):
            row_arrived(0, slot)
            values_at[half][0][c, slot - 2 * half] = v_raw[slot].reshape(2, BLK, HD)
        for ln in (2, 0, 1):
            x_copy(0, ln, half).start()
        c_copy(0, 0, half).start()

    def pass_values(half):
        for ln in (0, 1, 2):
            x_arrived(0, ln, half)
            c_copy(0, 1 + ln, half).start()

    def scaled(raw, scale, row, gain):
        scale = jnp.broadcast_to(scale[row : row + 1, :], (TOK, HD)).T
        gain = gain[pl.ds(pl.multiple_of(head * HD, HD), HD)].reshape(1, HD)
        return (raw.astype(F32) * scale * gain).astype(BF16)

    def own_scales(half):
        for i in range(2):
            slot = 2 * half + i

            @pl.when(slot != slot_mine)
            def _():
                arrived(inv_own.at[4 * part + slot], io_recv.at[4 * part + slot])

    def other_scales():
        for i in range(4):
            arrived(inv_own.at[4 - 4 * part + i], io_recv.at[4 - 4 * part + i])

    def norm_keys(col, half):
        if col > 0:
            x_arrived(1, col - 1, half)
        for i in range(2):
            slot = 2 * half + i
            if col == 0:
                scale = inv_own[4 * part + slot]
            else:
                arrived(inv_buf.at[col - 1, slot], i_recv.at[col - 1, slot])
                scale = inv_buf[col - 1, slot]
            keys = scaled(k_raw[col, slot], scale, 1, kg_in)
            keys_at[half][col][c, i] = keys.reshape(2, BLK, HD)
        c_copy(1, col, half).start()

    def norm_query(zz):
        @pl.when(zz != z)
        def _():
            arrived(q_raw.at[zz], q_recv.at[zz])

        @pl.when(zz == z)
        def _():
            own_copy(2, 0).wait()

        qbuf[zz] = scaled(q_raw[zz], inv_own[zz], 0, qg_in)

    @pl.when(active)
    def _():
        spread_own(0)
        spread_own(1)

    @pl.when(part == 0)
    def _():
        for i in range(3, 6):
            await_row(ROWS[i])
            queries_to(i)

    for yy in range(ny):

        @pl.when(yy != y)
        def _():
            arrived(sbuf.at[yy], s_recv.at[yy])

    for cp in late_loads:
        cp.wait()
    totals = sbuf[0]
    for i in range(1, ny):
        totals = totals + sbuf[i]
    inv = lax.rsqrt(totals / (NH * HD * ny) + EPS)

    isc[...] = inv

    def inv_copy(h, d):
        col = (None, 0, 2, 1)[d]
        return remote(
            isc, inv_buf.at[col, slot_mine], i_send.at[h, d], i_recv.at[col, slot_mine],
            dev(h + 4 * part, lax.rem(x + d, NX), c),
        )

    def io_copy(i):
        return remote(isc, inv_own.at[z], io_send.at[i], io_recv.at[z], dev(ROWS[i], x, c))

    inv_own[z] = inv
    for i, row in enumerate(ROWS):

        @pl.when((row != z) & (part == i // NH))
        def _():
            io_copy(i).start()

    for h in range(NH):
        for d in (2, 1, 3):
            inv_copy(h, d).start()
    for i, row in enumerate(ROWS):

        @pl.when((row != z) & (part != i // NH))
        def _():
            io_copy(i).start()

    @pl.when(part == 1)
    def _():
        for i in range(6):
            queries_to(i)

    lane = lax.broadcasted_iota(jnp.int32, (1, HD), 1)
    lane_sq = lax.broadcasted_iota(jnp.int32, (TOK, HD), 1)

    def o_copy(zz):
        return remote(
            ost.at[zz], obuf.at[head, part], o_send.at[zz], o_recv.at[head, part], dev(zz, x, c)
        )

    def t_copy(zz):
        return remote(
            stst.at[zz], stb.at[head, part], t_send.at[zz], t_recv.at[head, part], dev(zz, x, c)
        )

    def band_slot(zz, d):
        j = zz * 8 + x * 2 + c + d
        zj = jnp.clip(j, 0, 63) // 8
        ok = (zj // 4 == part) & (j >= 0) & (j <= 63)
        return lax.rem(zj, 4), jnp.where(ok, 0.0, MASKED).astype(F32)

    def second(of, col, core, slot):
        at = lax.rem(slot, 2)
        return jnp.where(slot < 2, of[0][col][core, at, 1], of[1][col][core, at, 1])

    def attend(half, pair, zz, band):
        key_parts, value_parts = [], []
        for col in (2 * pair, 2 * pair + 1):
            for core in range(NC):
                for i in range(2):
                    owner = (4 * part + 2 * half + i) * 8 + colx[col] * 2 + core
                    pick = jnp.maximum(fsm[zz, 0, owner], 0)
                    key_parts.append(keys_at[half][col][core, i, pick])
                    value_parts.append(values_at[half][col][core, i, pick])
        add = [bias[2 * half + pair, pl.ds(zz, 1), :]]
        if band:
            slot, own = band_slot(zz, 0)
            slot_two, two = band_slot(zz, 1 - 2 * c)
            slot_three, three = band_slot(zz, 2 * c - 1)
            for of, parts in ((keys_at, key_parts), (values_at, value_parts)):
                parts.append(second(of, 0, c, slot))
                parts.append(second(of, 0, 1 - c, slot_two))
                last = jnp.where(c == 0, second(of, 1, 1, slot_three), second(of, 2, 0, slot_three))
                parts += [last, last]
            add.append(jnp.where(lane < BLK, own, two))
            add.append(jnp.where(lane < BLK, three, MASKED))
        keys = jnp.concatenate(key_parts, axis=0)
        values = jnp.concatenate(value_parts, axis=0)
        scores = lax.dot_general(
            qbuf[zz], keys, (((1,), (1,)), ((), ())), preferred_element_type=F32
        ) + jnp.concatenate(add, axis=1)
        return [scores[:, i * HD : (i + 1) * HD] for i in range(scores.shape[1] // HD)], values

    def chunk(half, pair, group):
        first, last = (half, pair) == (0, 0), (half, pair) == (1, 1)
        blocks = [group * GROUP + i for i in range(GROUP)]
        scored = [attend(half, pair, zz, last) for zz in blocks]
        tops, fades, totals_of, contexts = [], [], [], []
        for zz, (tiles, _) in zip(blocks, scored):
            top = functools.reduce(jnp.maximum, tiles)
            top = jnp.broadcast_to(jnp.max(top, axis=1, keepdims=True), (TOK, HD))
            if not first:
                old = m_ref[zz]
                top = jnp.maximum(old, top)
                fades.append(jnp.exp2((old - top) * COEF))
            tops.append(top)
        for i, (zz, (tiles, values)) in enumerate(zip(blocks, scored)):
            tiles = [jnp.exp2((t - tops[i]) * COEF) for t in tiles]
            total = functools.reduce(jnp.add, tiles)
            weights = jnp.concatenate([t.astype(BF16) for t in tiles], axis=1)
            context = jnp.dot(weights, values, preferred_element_type=F32)
            if not first:
                total = l_ref[zz] * fades[i] + total
                context = acc_ref[zz] * fades[i] + context
            totals_of.append(total)
            contexts.append(context)
        if not last:
            for zz, top, total, context in zip(blocks, tops, totals_of, contexts):
                m_ref[zz] = top
                l_ref[zz] = total
                acc_ref[zz] = context
            return
        results = []
        for top, total, context in zip(tops, totals_of, contexts):
            total = jnp.broadcast_to(jnp.sum(total, axis=1, keepdims=True), (TOK, HD))
            stats = jnp.where(lane_sq == 0, top, total).T[0:8]
            results.append(((context / total).astype(BF16), stats))
        for zz, (context, stats) in zip(blocks, results):
            ost[zz] = context
            stst[zz] = stats
        for zz, (context, stats) in zip(blocks, results):

            @pl.when(zz == z)
            def _():
                obuf[head, part] = context
                stb[head, part] = stats

            @pl.when(zz != z)
            def _():
                o_copy(zz).start()
                t_copy(zz).start()

    def far_arrived(zz):
        @pl.when(zz != z)
        def _():
            arrived(fbuf.at[zz], f_recv.at[zz])

    @pl.when(active)
    def _():
        pass_values(0)

        for zz in range(NZ):
            far_arrived(zz)
        cp = pltpu.make_async_copy(fbuf, fsm, fsm_sem)
        cp.start()
        far = fbuf[:, 0, 0:64]
        block = lax.broadcasted_iota(jnp.int32, (NZ, 64), 0) * 8 + x * 2 + c
        other = lax.broadcasted_iota(jnp.int32, (NZ, 64), 1)
        valid = jnp.where((far >= 0) | (jnp.abs(block - other) <= 1), 1.0, 0.0).astype(BF16)
        at = lax.broadcasted_iota(jnp.int32, (64, 512), 1) // BLK
        src = lax.broadcasted_iota(jnp.int32, (64, 512), 0)
        for half in range(2):
            for pair in range(2):
                zsrc = 4 * part + 2 * half + lax.rem(at, 2)
                column = jnp.where(at < 4, colx[2 * pair], colx[2 * pair + 1])
                spread = (src == zsrc * 8 + column * 2 + lax.rem(at // 2, 2)).astype(F32)
                hit = jnp.dot(valid, spread.astype(BF16), preferred_element_type=F32)
                bias[2 * half + pair] = jnp.where(hit > 0.5, 0.0, MASKED)
        cp.wait()

        pass_values(1)

        def groups(group, carry):
            @pl.when((group == 0) & (part == 0))
            def _():
                own_scales(0)
                for col in range(NX):
                    norm_keys(col, 0)
                own_scales(1)

            @pl.when(group != part)
            def _():
                other_scales()

            for i in range(GROUP):
                norm_query(group * GROUP + i)

            @pl.when((group == 0) & (part == 1))
            def _():
                own_scales(0)
                for col in range(NX):
                    norm_keys(col, 0)
                own_scales(1)

            @pl.when(group == 0)
            def _():
                for col in range(NX):
                    c_arrived(0, col, 0)
                    c_arrived(0, col, 1)
                for col in range(NX):
                    norm_keys(col, 1)
                for col in range(NX):
                    c_arrived(1, col, 0)

            chunk(0, 0, group)

            chunk(0, 1, group)

            @pl.when(group == 0)
            def _():
                for col in range(NX):
                    c_arrived(1, col, 1)

            chunk(1, 0, group)
            chunk(1, 1, group)
            return carry

        lax.fori_loop(0, NZ // GROUP, groups, 0)

    start = tm * TOK
    frame = start // FRAME_TOK
    after = jnp.minimum(frame + 1, 5)
    steps = lax.broadcasted_iota(jnp.int32, gate_in.shape, 0)

    def gate_of(step):
        return jnp.sum(jnp.where(steps == step, gate_in[...], 0.0), axis=0, keepdims=True)

    gate_a, gate_b = gate_of(frame_ref[frame]), gate_of(frame_ref[after])
    edge = (frame + 1) * FRAME_TOK - start
    before = lax.broadcasted_iota(jnp.int32, (TOK, HD), 0) < edge
    for h in range(NH):
        for p in range(2):

            @pl.when(h + 4 * p != z)
            def _():
                arrived(obuf.at[h, p], o_recv.at[h, p])
                arrived(stb.at[h, p], t_recv.at[h, p])

        span = slice(h * HD, (h + 1) * HD)
        one, two = stb[h, 0], stb[h, 1]
        top = jnp.maximum(one[0:1], two[0:1])
        weight_one = one[1:2] * jnp.exp2((one[0:1] - top) * COEF)
        weight_two = two[1:2] * jnp.exp2((two[0:1] - top) * COEF)
        share = weight_one / (weight_one + weight_two)
        share = jnp.broadcast_to(share, (TOK, HD)).T
        context = obuf[h, 0].astype(F32) * share + obuf[h, 1].astype(F32) * (1.0 - share)
        gate = jnp.where(before, gate_a[:, span], gate_b[:, span])
        out_ref[:, span] = (context * gate).astype(BF16)

    for yy in range(ny):

        @pl.when(yy != y)
        def _():
            s_copy(yy).wait_send()

    for h in range(NH):
        for d in range(1, NX):
            inv_copy(h, d).wait_send()

        @pl.when(h + 4 * part != z)
        def _():
            for cp in row_copies(h):
                cp.wait_send()

    for i, row in enumerate(ROWS):

        @pl.when(row != z)
        def _():
            f_copy(i).wait_send()
            q_copy(i).wait_send()
            io_copy(i).wait_send()

    @pl.when(active)
    def _():
        for t in range(2):
            for ln in range(3):
                for half in range(2):
                    x_copy(t, ln, half).wait_send()
            for col in range(4):
                for half in range(2):
                    c_copy(t, col, half).wait_send()
        for zz in range(NZ):

            @pl.when(zz != z)
            def _():
                o_copy(zz).wait_send()
                t_copy(zz).wait_send()


def solution(mesh):
    ny = mesh.shape["head"]
    dma = pltpu.SemaphoreType.DMA
    vmem = pltpu.VMEM

    def local(query, key, value, query_gain, key_gain, gate_table, frame_step, far_blocks):
        whole = pl.BlockSpec(memory_space=pltpu.VMEM)
        hbm = pl.BlockSpec(memory_space=pltpu.HBM)
        width = NH * HD
        return pl.pallas_call(
            functools.partial(kernel, ny),
            out_shape=pltpu.VMEM((TOK, width), BF16),
            in_specs=[hbm] * 6 + [pl.BlockSpec(memory_space=pltpu.SMEM), whole],
            out_specs=whole,
            scratch_shapes=[
                vmem((TOK, width), BF16),
                vmem((TOK, width), BF16),
                vmem((width,), F32),
                vmem((width,), F32),
                vmem((50, width), F32),
                vmem((NZ, TOK, HD), BF16),
                vmem((NX, 4, TOK, HD), BF16),
                vmem((4, TOK, HD), BF16),
                vmem((8, TOK), F32),
                vmem((NZ, 8, TOK), F32),
                vmem((NX - 1, 4, 8, TOK), F32),
                vmem((NZ, TOK, HD), BF16),
                vmem((8, 128), jnp.int32),
                vmem((NZ, 8, 128), jnp.int32),
                pltpu.SMEM((NZ, 8, 128), jnp.int32),
                vmem((8, TOK), F32),
                vmem((ny, 8, TOK), F32),
                vmem((4, NZ, 512), F32),
                vmem((NZ, TOK, HD), F32),
                vmem((NZ, TOK, HD), F32),
                vmem((NZ, TOK, HD), F32),
                vmem((NZ, TOK, HD), BF16),
                vmem((NZ, 8, TOK), F32),
                vmem((NH, 2, TOK, HD), BF16),
                vmem((NH, 2, 8, TOK), F32),
                *[vmem((NC, 2, 2, BLK, HD), BF16)] * 16,
                dma((5,)), dma((3,)), dma, pltpu.SemaphoreType.REGULAR((NZ,)),
                pltpu.SemaphoreType.REGULAR((ny,)),
                dma((ny,)), dma((ny,)), dma((6,)), dma((NZ,)), dma((6,)), dma((NZ,)),
                dma((2, 3)), dma((2, 4)), dma((6,)), dma((NZ,)), dma((3, 4)), dma((3, 4)),
                dma((2, 3, 2)), dma((2, 3, 2)),
                dma((2, 4, 2)), dma((2, 4, 2)),
                dma((NZ,)), dma((NH, 2)), dma((NZ,)), dma((NH, 2)),
            ],
            compiler_params=pltpu.CompilerParams(
                collective_id=0, has_side_effects=True, vmem_limit_bytes=56 * 2**20
            ),
            name="attend",
        )(
            query, key, value, query_gain, key_gain,
            gate_table, frame_step, far_blocks,
        )

    return jax.shard_map(
        local,
        mesh=mesh,
        in_specs=(
            P("tm", "head"),
            P("tm", "head"),
            P("tm", "head"),
            P("head"),
            P("head"),
            P(None, "head"),
            P(),
            P("tm", None),
        ),
        out_specs=P("tm", "head"),
        check_vma=False,
    )
```

```python
import functools

import jax
import jax.numpy as jnp
from jax import lax
from jax.experimental import pallas as pl
from jax.experimental.pallas import tpu as pltpu
from jax.sharding import PartitionSpec as P

HD = 128
TOK = 128
BLK = 64
FRAME_TOK = 1560
NZ, NX, NC = 8, 4, 2
NH = 3
EPS = 1e-06
MASKED = -1e30
GROUP = 4
LOG2E = 1.4426950408889634
COEF = HD**-0.5 * LOG2E
MESH = pl.DeviceIdType.MESH
TWO = pl.ds(0, 2)
BF16 = jnp.bfloat16
F32 = jnp.float32

ROWS = (0, 1, 2, 4, 5, 6)


def kernel(
    ny,
    q_hbm, k_hbm, v_hbm, qg_hbm, kg_hbm, gate_hbm, frame_ref, far_ref,
    out_ref,
    qin, kin, qg_in, kg_in, gate_in, q_raw, k_raw, v_raw, isc, inv_own, inv_buf, qbuf,
    fst, fbuf, fsm, sst, sbuf, bias, m_ref, l_ref, acc_ref, ost, stst, obuf, stb,
    *rest,
):
    keys_at, values_at = (rest[0:4], rest[4:8]), (rest[8:12], rest[12:16])
    (
        load_sem, own_sem, fsm_sem, hello, hello_y,
        s_send, s_recv, f_send, f_recv, q_send, q_recv,
        p1_send, p1_recv, io_send, io_recv, i_send, i_recv, x_send, x_recv, c_send, c_recv,
        o_send, o_recv, t_send, t_recv,
    ) = rest[16:]
    tm = lax.axis_index("tm")
    y = lax.axis_index("head")
    c = lax.rem(tm, NC)
    x = lax.rem(tm // NC, NX)
    z = tm // (NC * NX)
    part, slot_mine = z // 4, lax.rem(z, 4)
    active = slot_mine < 3
    head = jnp.minimum(slot_mine, 2)
    xl, xr = lax.rem(x + 3, NX), lax.rem(x + 1, NX)
    colx = (x, xl, xr, lax.rem(x + 2, NX))

    def dev(zz, xx, cc):
        return (zz * (NX * NC) + xx * NC + cc, y)

    def remote(src, dst, ss, rs, target):
        return pltpu.make_async_remote_copy(
            src_ref=src, dst_ref=dst, send_sem=ss, recv_sem=rs,
            device_id=target, device_id_type=MESH,
        )

    loads = [
        pltpu.make_async_copy(s, d, load_sem.at[i])
        for i, (s, d) in enumerate(((k_hbm, kin), (q_hbm, qin)))
    ]
    late_loads = [
        pltpu.make_async_copy(s, d, load_sem.at[2 + i])
        for i, (s, d) in enumerate(((qg_hbm, qg_in), (kg_hbm, kg_in), (gate_hbm, gate_in)))
    ]
    for cp in loads + late_loads:
        cp.start()

    barrier = pltpu.get_barrier_semaphore()

    def greet(target):
        pl.semaphore_signal(barrier, inc=1, device_id=target, device_id_type=MESH)

    for d in range(1, NX):
        greet(dev(z, lax.rem(x + d, NX), c))
    greet(dev(z, x, 1 - c))
    for yy in range(1, ny):

        @pl.when(yy > y)
        def _():
            greet((tm, yy))

    for zz in range(1, NZ):

        @pl.when(zz > z)
        def _():
            greet(dev(zz, x, c))

        @pl.when((zz > z) & (zz // 4 == part))
        def _():
            for d in range(1, NX):
                greet(dev(zz, lax.rem(x + d, NX), c))

    pl.semaphore_wait(barrier, NX + z + 3 * slot_mine + y)

    for zz in range(NZ - 1):

        @pl.when(active & (zz < z))
        def _():
            pl.semaphore_signal(hello.at[z], inc=1, device_id=dev(zz, x, c), device_id_type=MESH)

    for yy in range(ny - 1):

        @pl.when(yy < y)
        def _():
            pl.semaphore_signal(hello_y.at[y], inc=1, device_id=(tm, yy), device_id_type=MESH)

    def await_row(row):
        @pl.when(row > z)
        def _():
            pl.semaphore_wait(hello.at[row], 1)

    def row_copies(h):
        row, cols = h + 4 * part, pl.ds(h * HD, HD)
        return [
            remote(
                ref.at[:, cols], dst, p1_send.at[t, h], p1_recv.at[t, slot_mine], dev(row, x, c)
            )
            for t, ref, dst in (
                (1, k_hbm, k_raw.at[0, slot_mine]),
                (0, v_hbm, v_raw.at[slot_mine]),
            )
        ]

    def own_copy(t, h):
        ref, dst = (
            (v_hbm, v_raw.at[slot_mine]), (k_hbm, k_raw.at[0, slot_mine]), (q_hbm, q_raw.at[z])
        )[t]
        return pltpu.make_async_copy(ref.at[:, pl.ds(h * HD, HD)], dst, own_sem.at[t])

    def f_copy(i):
        return remote(fst, fbuf.at[z], f_send.at[i], f_recv.at[z], dev(ROWS[i], x, c))

    def q_copy(i):
        source = q_hbm.at[:, pl.ds(i % NH * HD, HD)]
        return remote(source, q_raw.at[z], q_send.at[i], q_recv.at[z], dev(ROWS[i], x, c))

    def far_to(i):
        @pl.when(ROWS[i] != z)
        def _():
            f_copy(i).start()

    def queries_to(i):
        @pl.when(ROWS[i] != z)
        def _():
            q_copy(i).start()

    far_row = jnp.concatenate([far_ref[...], jnp.full((1, 64), -1, jnp.int32)], axis=1)
    fst[...] = jnp.broadcast_to(far_row, (8, 128))
    fbuf[z] = fst[...]
    def keys_to(i):
        row = ROWS[i]

        @pl.when(row != z)
        def _():
            for cp in row_copies(i % NH):
                cp.start()

        @pl.when(row == z)
        def _():
            for t in range(3):
                own_copy(t, i % NH).start()

    for i in range(6):

        @pl.when((part == i // NH) & (ROWS[i] <= z))
        def _():
            keys_to(i)

    for cp in loads:
        cp.wait()

    def square_sums(ref):
        f = ref[...].astype(F32)
        sq = f * f
        sq = sq[:, 0:HD] + sq[:, HD : 2 * HD] + sq[:, 2 * HD : 3 * HD]
        return jnp.sum(sq.T, axis=0, keepdims=True)

    sst[...] = jnp.concatenate(
        [square_sums(qin), square_sums(kin), jnp.zeros((6, TOK), F32)], axis=0
    )
    sbuf[y] = sst[...]

    def s_copy(yy):
        return remote(sst.at[TWO], sbuf.at[y, TWO], s_send.at[yy], s_recv.at[y], (tm, yy))

    for yy in range(ny - 1):

        @pl.when(yy < y)
        def _():
            s_copy(yy).start()

    for i in range(6):

        @pl.when((part == i // NH) & (ROWS[i] > z))
        def _():
            await_row(ROWS[i])
            keys_to(i)

    for p in range(2):

        @pl.when(part == p)
        def _():
            for i in range(3 + 3 * p):
                far_to(i)

    @pl.when(part == 0)
    def _():
        for i in range(3):
            queries_to(i)

    for yy in range(1, ny):

        @pl.when(yy > y)
        def _():
            pl.semaphore_wait(hello_y.at[yy], 1)
            s_copy(yy).start()

    def arrived(ref, sem):
        remote(ref, ref, s_send.at[0], sem, dev(z, x, 1 - c)).wait_recv()

    def row_arrived(t, slot):
        ref = (v_raw.at[slot], k_raw.at[0, slot])[t]

        @pl.when(slot == slot_mine)
        def _():
            own_copy(t, 0).wait()

        @pl.when(slot != slot_mine)
        def _():
            arrived(ref, p1_recv.at[t, slot])

    def k_half(col, half):
        return k_raw.at[col, pl.ds(2 * half, 2)]

    def x_copy(t, lane, half):
        if t == 1:
            src, dst = k_half(0, half), k_half(1 + lane, half)
        else:
            src, dst = values_at[half][0].at[c], values_at[half][1 + lane].at[c]
        return remote(
            src, dst, x_send.at[t, lane, half], x_recv.at[t, lane, half],
            dev(z, lax.rem(x + (1, 3, 2)[lane], NX), c),
        )

    def x_arrived(t, lane, half):
        x_copy(t, lane, half).wait_recv()

    def c_copy(t, col, half):
        ref = (values_at, keys_at)[t][half][col].at[c]
        return remote(
            ref, ref, c_send.at[t, col, half], c_recv.at[t, col, half], dev(z, x, 1 - c)
        )

    def c_arrived(t, col, half):
        arrived((values_at, keys_at)[t][half][col].at[1 - c], c_recv.at[t, col, half])

    def spread_own(half):
        for slot in (2 * half, 2 * half + 1):
            row_arrived(1, slot)
        for ln in (2, 0, 1):
            x_copy(1, ln, half).start()
        for slot in (2 * half, 2 * half + 1):
            row_arrived(0, slot)
            values_at[half][0][c, slot - 2 * half] = v_raw[slot].reshape(2, BLK, HD)
        for ln in (2, 0, 1):
            x_copy(0, ln, half).start()
        c_copy(0, 0, half).start()

    def pass_values(half):
        for ln in (0, 1, 2):
            x_arrived(0, ln, half)
            c_copy(0, 1 + ln, half).start()

    def scaled(raw, scale, row, gain):
        scale = jnp.broadcast_to(scale[row : row + 1, :], (TOK, HD)).T
        gain = gain[pl.ds(pl.multiple_of(head * HD, HD), HD)].reshape(1, HD)
        return (raw.astype(F32) * scale * gain).astype(BF16)

    def own_scales(half):
        for i in range(2):
            slot = 2 * half + i

            @pl.when(slot != slot_mine)
            def _():
                arrived(inv_own.at[4 * part + slot, TWO], io_recv.at[4 * part + slot])

    def other_scales():
        for i in range(4):
            arrived(inv_own.at[4 - 4 * part + i, TWO], io_recv.at[4 - 4 * part + i])

    def norm_keys(col, half):
        if col > 0:
            x_arrived(1, col - 1, half)
        for i in range(2):
            slot = 2 * half + i
            if col == 0:
                scale = inv_own[4 * part + slot]
            else:
                arrived(inv_buf.at[col - 1, slot, TWO], i_recv.at[col - 1, slot])
                scale = inv_buf[col - 1, slot]
            keys = scaled(k_raw[col, slot], scale, 1, kg_in)
            keys_at[half][col][c, i] = keys.reshape(2, BLK, HD)
        c_copy(1, col, half).start()

    def norm_query(zz):
        @pl.when(zz != z)
        def _():
            arrived(q_raw.at[zz], q_recv.at[zz])

        @pl.when(zz == z)
        def _():
            own_copy(2, 0).wait()

        qbuf[zz] = scaled(q_raw[zz], inv_own[zz], 0, qg_in)

    @pl.when(active)
    def _():
        spread_own(0)
        spread_own(1)

    @pl.when(part == 1)
    def _():
        for i in range(6):
            queries_to(i)

    @pl.when(part == 0)
    def _():
        for i in range(3, 6):
            await_row(ROWS[i])
            far_to(i)
            queries_to(i)

    for yy in range(ny):

        @pl.when(yy != y)
        def _():
            arrived(sbuf.at[yy, TWO], s_recv.at[yy])

    for cp in late_loads:
        cp.wait()
    totals = sbuf[0]
    for i in range(1, ny):
        totals = totals + sbuf[i]
    inv = lax.rsqrt(totals / (NH * HD * ny) + EPS)

    isc[...] = inv

    def inv_copy(h, d):
        col = (None, 0, 2, 1)[d]
        return remote(
            isc.at[TWO], inv_buf.at[col, slot_mine, TWO], i_send.at[h, d], i_recv.at[col, slot_mine],
            dev(h + 4 * part, lax.rem(x + d, NX), c),
        )

    def io_copy(i):
        return remote(
            isc.at[TWO], inv_own.at[z, TWO], io_send.at[i], io_recv.at[z], dev(ROWS[i], x, c)
        )

    inv_own[z] = inv
    for i, row in enumerate(ROWS):

        @pl.when((row != z) & (part == i // NH))
        def _():
            io_copy(i).start()

    for h in range(NH):
        for d in (2, 1, 3):
            inv_copy(h, d).start()
    for i, row in enumerate(ROWS):

        @pl.when((row != z) & (part != i // NH))
        def _():
            io_copy(i).start()

    lane = lax.broadcasted_iota(jnp.int32, (1, HD), 1)
    lane_sq = lax.broadcasted_iota(jnp.int32, (TOK, HD), 1)

    def o_copy(zz):
        return remote(
            ost.at[zz], obuf.at[head, part], o_send.at[zz], o_recv.at[head, part], dev(zz, x, c)
        )

    def t_copy(zz):
        return remote(
            stst.at[zz, TWO], stb.at[head, part, TWO], t_send.at[zz], t_recv.at[head, part], dev(zz, x, c)
        )

    def band_slot(zz, d):
        j = zz * 8 + x * 2 + c + d
        zj = jnp.clip(j, 0, 63) // 8
        ok = (zj // 4 == part) & (j >= 0) & (j <= 63)
        return lax.rem(zj, 4), jnp.where(ok, 0.0, MASKED).astype(F32)

    def second(of, col, core, slot):
        at = lax.rem(slot, 2)
        return jnp.where(slot < 2, of[0][col][core, at, 1], of[1][col][core, at, 1])

    def attend(half, pair, zz, band):
        key_parts, value_parts = [], []
        for col in (2 * pair, 2 * pair + 1):
            for core in range(NC):
                for i in range(2):
                    owner = (4 * part + 2 * half + i) * 8 + colx[col] * 2 + core
                    pick = jnp.maximum(fsm[zz, 0, owner], 0)
                    key_parts.append(keys_at[half][col][core, i, pick])
                    value_parts.append(values_at[half][col][core, i, pick])
        add = [bias[2 * half + pair, pl.ds(zz, 1), :]]
        if band:
            slot, own = band_slot(zz, 0)
            slot_two, two = band_slot(zz, 1 - 2 * c)
            slot_three, three = band_slot(zz, 2 * c - 1)
            for of, parts in ((keys_at, key_parts), (values_at, value_parts)):
                parts.append(second(of, 0, c, slot))
                parts.append(second(of, 0, 1 - c, slot_two))
                last = jnp.where(c == 0, second(of, 1, 1, slot_three), second(of, 2, 0, slot_three))
                parts += [last, last]
            add.append(jnp.where(lane < BLK, own, two))
            add.append(jnp.where(lane < BLK, three, MASKED))
        keys = jnp.concatenate(key_parts, axis=0)
        values = jnp.concatenate(value_parts, axis=0)
        scores = lax.dot_general(
            qbuf[zz], keys, (((1,), (1,)), ((), ())), preferred_element_type=F32
        ) + jnp.concatenate(add, axis=1)
        return [scores[:, i * HD : (i + 1) * HD] for i in range(scores.shape[1] // HD)], values

    def chunk(half, pair, group):
        first, last = (half, pair) == (0, 0), (half, pair) == (1, 1)
        blocks = [group * GROUP + i for i in range(GROUP)]
        scored = [attend(half, pair, zz, last) for zz in blocks]
        tops, fades, totals_of, contexts = [], [], [], []
        for zz, (tiles, _) in zip(blocks, scored):
            top = functools.reduce(jnp.maximum, tiles)
            top = jnp.broadcast_to(jnp.max(top, axis=1, keepdims=True), (TOK, HD))
            if not first:
                old = m_ref[zz]
                top = jnp.maximum(old, top)
                fades.append(jnp.exp2((old - top) * COEF))
            tops.append(top)
        for i, (zz, (tiles, values)) in enumerate(zip(blocks, scored)):
            tiles = [jnp.exp2((t - tops[i]) * COEF) for t in tiles]
            total = functools.reduce(jnp.add, tiles)
            weights = jnp.concatenate([t.astype(BF16) for t in tiles], axis=1)
            context = jnp.dot(weights, values, preferred_element_type=F32)
            if not first:
                total = l_ref[zz] * fades[i] + total
                context = acc_ref[zz] * fades[i] + context
            totals_of.append(total)
            contexts.append(context)
        if not last:
            for zz, top, total, context in zip(blocks, tops, totals_of, contexts):
                m_ref[zz] = top
                l_ref[zz] = total
                acc_ref[zz] = context
            return
        results = []
        for top, total, context in zip(tops, totals_of, contexts):
            total = jnp.broadcast_to(jnp.sum(total, axis=1, keepdims=True), (TOK, HD))
            stats = jnp.where(lane_sq == 0, top, total).T[0:8]
            results.append(((context / total).astype(BF16), stats))
        for zz, (context, stats) in zip(blocks, results):
            ost[zz] = context
            stst[zz] = stats
        for zz, (context, stats) in zip(blocks, results):

            @pl.when(zz == z)
            def _():
                obuf[head, part] = context
                stb[head, part] = stats

            @pl.when(zz != z)
            def _():
                o_copy(zz).start()
                t_copy(zz).start()

    def far_arrived(zz):
        @pl.when(zz != z)
        def _():
            arrived(fbuf.at[zz], f_recv.at[zz])

    @pl.when(active)
    def _():
        pass_values(0)

        for zz in range(NZ):
            far_arrived(zz)
        cp = pltpu.make_async_copy(fbuf, fsm, fsm_sem)
        cp.start()
        far = fbuf[:, 0, 0:64]
        block = lax.broadcasted_iota(jnp.int32, (NZ, 64), 0) * 8 + x * 2 + c
        other = lax.broadcasted_iota(jnp.int32, (NZ, 64), 1)
        valid = jnp.where((far >= 0) | (jnp.abs(block - other) <= 1), 1.0, 0.0).astype(BF16)
        at = lax.broadcasted_iota(jnp.int32, (64, 512), 1) // BLK
        src = lax.broadcasted_iota(jnp.int32, (64, 512), 0)
        for half in range(2):
            for pair in range(2):
                zsrc = 4 * part + 2 * half + lax.rem(at, 2)
                column = jnp.where(at < 4, colx[2 * pair], colx[2 * pair + 1])
                spread = (src == zsrc * 8 + column * 2 + lax.rem(at // 2, 2)).astype(F32)
                hit = jnp.dot(valid, spread.astype(BF16), preferred_element_type=F32)
                bias[2 * half + pair] = jnp.where(hit > 0.5, 0.0, MASKED)
        cp.wait()

        def groups(group, carry):
            @pl.when((group == 0) & (part == 0))
            def _():
                own_scales(0)
                own_scales(1)

            @pl.when(group != part)
            def _():
                other_scales()

            for i in range(GROUP):
                norm_query(group * GROUP + i)

            @pl.when((group == 0) & (part == 1))
            def _():
                own_scales(0)

            @pl.when(group == 0)
            def _():
                for col in range(NX):
                    norm_keys(col, 0)
                for col in range(NX):
                    c_arrived(0, col, 0)
                    c_arrived(1, col, 0)

            chunk(0, 0, group)

            @pl.when((group == 0) & (part == 1))
            def _():
                own_scales(1)

            @pl.when(group == 0)
            def _():
                for col in range(NX):
                    norm_keys(col, 1)
                pass_values(1)

            chunk(0, 1, group)

            @pl.when(group == 0)
            def _():
                for col in range(NX):
                    c_arrived(0, col, 1)
                    c_arrived(1, col, 1)

            chunk(1, 0, group)
            chunk(1, 1, group)
            return carry

        lax.fori_loop(0, NZ // GROUP, groups, 0)

    start = tm * TOK
    frame = start // FRAME_TOK
    after = jnp.minimum(frame + 1, 5)
    steps = lax.broadcasted_iota(jnp.int32, gate_in.shape, 0)

    def gate_of(step):
        return jnp.sum(jnp.where(steps == step, gate_in[...], 0.0), axis=0, keepdims=True)

    gate_a, gate_b = gate_of(frame_ref[frame]), gate_of(frame_ref[after])
    edge = (frame + 1) * FRAME_TOK - start
    before = lax.broadcasted_iota(jnp.int32, (TOK, HD), 0) < edge
    for h in range(NH):
        for p in range(2):

            @pl.when(h + 4 * p != z)
            def _():
                arrived(obuf.at[h, p], o_recv.at[h, p])
                arrived(stb.at[h, p, TWO], t_recv.at[h, p])

        span = slice(h * HD, (h + 1) * HD)
        one, two = stb[h, 0], stb[h, 1]
        top = jnp.maximum(one[0:1], two[0:1])
        weight_one = one[1:2] * jnp.exp2((one[0:1] - top) * COEF)
        weight_two = two[1:2] * jnp.exp2((two[0:1] - top) * COEF)
        share = weight_one / (weight_one + weight_two)
        share = jnp.broadcast_to(share, (TOK, HD)).T
        context = obuf[h, 0].astype(F32) * share + obuf[h, 1].astype(F32) * (1.0 - share)
        gate = jnp.where(before, gate_a[:, span], gate_b[:, span])
        out_ref[:, span] = (context * gate).astype(BF16)

    for yy in range(ny):

        @pl.when(yy != y)
        def _():
            s_copy(yy).wait_send()

    for h in range(NH):
        for d in range(1, NX):
            inv_copy(h, d).wait_send()

        @pl.when(h + 4 * part != z)
        def _():
            for cp in row_copies(h):
                cp.wait_send()

    for i, row in enumerate(ROWS):

        @pl.when(row != z)
        def _():
            f_copy(i).wait_send()
            q_copy(i).wait_send()
            io_copy(i).wait_send()

    @pl.when(active)
    def _():
        for t in range(2):
            for ln in range(3):
                for half in range(2):
                    x_copy(t, ln, half).wait_send()
            for col in range(4):
                for half in range(2):
                    c_copy(t, col, half).wait_send()
        for zz in range(NZ):

            @pl.when(zz != z)
            def _():
                o_copy(zz).wait_send()
                t_copy(zz).wait_send()


def solution(mesh):
    ny = mesh.shape["head"]
    dma = pltpu.SemaphoreType.DMA
    vmem = pltpu.VMEM

    def local(query, key, value, query_gain, key_gain, gate_table, frame_step, far_blocks):
        whole = pl.BlockSpec(memory_space=pltpu.VMEM)
        hbm = pl.BlockSpec(memory_space=pltpu.HBM)
        width = NH * HD
        return pl.pallas_call(
            functools.partial(kernel, ny),
            out_shape=pltpu.VMEM((TOK, width), BF16),
            in_specs=[hbm] * 6 + [pl.BlockSpec(memory_space=pltpu.SMEM), whole],
            out_specs=whole,
            scratch_shapes=[
                vmem((TOK, width), BF16),
                vmem((TOK, width), BF16),
                vmem((width,), F32),
                vmem((width,), F32),
                vmem((50, width), F32),
                vmem((NZ, TOK, HD), BF16),
                vmem((NX, 4, TOK, HD), BF16),
                vmem((4, TOK, HD), BF16),
                vmem((8, TOK), F32),
                vmem((NZ, 8, TOK), F32),
                vmem((NX - 1, 4, 8, TOK), F32),
                vmem((NZ, TOK, HD), BF16),
                vmem((8, 128), jnp.int32),
                vmem((NZ, 8, 128), jnp.int32),
                pltpu.SMEM((NZ, 8, 128), jnp.int32),
                vmem((8, TOK), F32),
                vmem((ny, 8, TOK), F32),
                vmem((4, NZ, 512), F32),
                vmem((NZ, TOK, HD), F32),
                vmem((NZ, TOK, HD), F32),
                vmem((NZ, TOK, HD), F32),
                vmem((NZ, TOK, HD), BF16),
                vmem((NZ, 8, TOK), F32),
                vmem((NH, 2, TOK, HD), BF16),
                vmem((NH, 2, 8, TOK), F32),
                *[vmem((NC, 2, 2, BLK, HD), BF16)] * 16,
                dma((5,)), dma((3,)), dma, pltpu.SemaphoreType.REGULAR((NZ,)),
                pltpu.SemaphoreType.REGULAR((ny,)),
                dma((ny,)), dma((ny,)), dma((6,)), dma((NZ,)), dma((6,)), dma((NZ,)),
                dma((2, 3)), dma((2, 4)), dma((6,)), dma((NZ,)), dma((3, 4)), dma((3, 4)),
                dma((2, 3, 2)), dma((2, 3, 2)),
                dma((2, 4, 2)), dma((2, 4, 2)),
                dma((NZ,)), dma((NH, 2)), dma((NZ,)), dma((NH, 2)),
            ],
            compiler_params=pltpu.CompilerParams(
                collective_id=0, has_side_effects=True, vmem_limit_bytes=56 * 2**20
            ),
            name="attend",
        )(
            query, key, value, query_gain, key_gain,
            gate_table, frame_step, far_blocks,
        )

    return jax.shard_map(
        local,
        mesh=mesh,
        in_specs=(
            P("tm", "head"),
            P("tm", "head"),
            P("tm", "head"),
            P("head"),
            P("head"),
            P(None, "head"),
            P(),
            P("tm", None),
        ),
        out_specs=P("tm", "head"),
        check_vma=False,
    )
```

```python
import functools

import jax
import jax.numpy as jnp
from jax import lax
from jax.experimental import pallas as pl
from jax.experimental.pallas import tpu as pltpu
from jax.sharding import PartitionSpec as P

HD = 128
TOK = 128
BLK = 64
FRAME_TOK = 1560
NZ, NX, NC = 8, 4, 2
NH = 3
EPS = 1e-06
MASKED = -1e30
GROUP = 4
LOG2E = 1.4426950408889634
COEF = HD**-0.5 * LOG2E
MESH = pl.DeviceIdType.MESH
TWO = pl.ds(0, 2)
BF16 = jnp.bfloat16
F32 = jnp.float32

ROWS = (0, 1, 2, 4, 5, 6)


def kernel(
    ny,
    q_hbm, k_hbm, v_hbm, qg_hbm, kg_hbm, gate_hbm, frame_ref, far_ref,
    out_ref,
    qin, kin, qg_in, kg_in, gate_in, q_raw, k_raw, v_raw, isc, inv_own, inv_buf, qbuf,
    fst, fbuf, fsm, sst, sbuf, bias, m_ref, l_ref, acc_ref, ost, stst, obuf, stb,
    *rest,
):
    keys_at, values_at = (rest[0:4], rest[4:8]), (rest[8:12], rest[12:16])
    (
        load_sem, own_sem, fsm_sem, hello, hello_y,
        s_send, s_recv, f_send, f_recv, q_send, q_recv,
        p1_send, p1_recv, io_send, io_recv, i_send, i_recv, x_send, x_recv, c_send, c_recv,
        o_send, o_recv, t_send, t_recv,
    ) = rest[16:]
    tm = lax.axis_index("tm")
    y = lax.axis_index("head")
    c = lax.rem(tm, NC)
    x = lax.rem(tm // NC, NX)
    z = tm // (NC * NX)
    part, slot_mine = z // 4, lax.rem(z, 4)
    active = slot_mine < 3
    head = jnp.minimum(slot_mine, 2)
    xl, xr = lax.rem(x + 3, NX), lax.rem(x + 1, NX)
    colx = (x, xl, xr, lax.rem(x + 2, NX))

    def dev(zz, xx, cc):
        return (zz * (NX * NC) + xx * NC + cc, y)

    def remote(src, dst, ss, rs, target):
        return pltpu.make_async_remote_copy(
            src_ref=src, dst_ref=dst, send_sem=ss, recv_sem=rs,
            device_id=target, device_id_type=MESH,
        )

    loads = [
        pltpu.make_async_copy(s, d, load_sem.at[i])
        for i, (s, d) in enumerate(((k_hbm, kin), (q_hbm, qin)))
    ]
    late_loads = [
        pltpu.make_async_copy(s, d, load_sem.at[2 + i])
        for i, (s, d) in enumerate(((qg_hbm, qg_in), (kg_hbm, kg_in), (gate_hbm, gate_in)))
    ]
    for cp in loads + late_loads:
        cp.start()

    barrier = pltpu.get_barrier_semaphore()

    def greet(target):
        pl.semaphore_signal(barrier, inc=1, device_id=target, device_id_type=MESH)

    for d in range(1, NX):
        greet(dev(z, lax.rem(x + d, NX), c))
    greet(dev(z, x, 1 - c))
    for yy in range(1, ny):

        @pl.when(yy > y)
        def _():
            greet((tm, yy))

    for zz in range(1, NZ):

        @pl.when(zz > z)
        def _():
            greet(dev(zz, x, c))

        @pl.when((zz > z) & (zz // 4 == part))
        def _():
            for d in range(1, NX):
                greet(dev(zz, lax.rem(x + d, NX), c))

    pl.semaphore_wait(barrier, NX + z + 3 * slot_mine + y)

    for zz in range(NZ - 1):

        @pl.when(active & (zz < z))
        def _():
            pl.semaphore_signal(hello.at[z], inc=1, device_id=dev(zz, x, c), device_id_type=MESH)

    for yy in range(ny - 1):

        @pl.when(yy < y)
        def _():
            pl.semaphore_signal(hello_y.at[y], inc=1, device_id=(tm, yy), device_id_type=MESH)

    def await_row(row):
        @pl.when(row > z)
        def _():
            pl.semaphore_wait(hello.at[row], 1)

    def row_copies(h):
        row, cols = h + 4 * part, pl.ds(h * HD, HD)
        return [
            remote(
                ref.at[:, cols], dst, p1_send.at[t, h], p1_recv.at[t, slot_mine], dev(row, x, c)
            )
            for t, ref, dst in (
                (1, k_hbm, k_raw.at[0, slot_mine]),
                (0, v_hbm, v_raw.at[slot_mine]),
            )
        ]

    def own_copy(t, h):
        ref, dst = (
            (v_hbm, v_raw.at[slot_mine]), (k_hbm, k_raw.at[0, slot_mine]), (q_hbm, q_raw.at[z])
        )[t]
        return pltpu.make_async_copy(ref.at[:, pl.ds(h * HD, HD)], dst, own_sem.at[t])

    def f_copy(i):
        return remote(fst, fbuf.at[z], f_send.at[i], f_recv.at[z], dev(ROWS[i], x, c))

    def q_copy(i):
        source = q_hbm.at[:, pl.ds(i % NH * HD, HD)]
        return remote(source, q_raw.at[z], q_send.at[i], q_recv.at[z], dev(ROWS[i], x, c))

    def far_to(i):
        @pl.when(ROWS[i] != z)
        def _():
            f_copy(i).start()

    def queries_to(i):
        @pl.when(ROWS[i] != z)
        def _():
            q_copy(i).start()

    far_row = jnp.concatenate([far_ref[...], jnp.full((1, 64), -1, jnp.int32)], axis=1)
    fst[...] = jnp.broadcast_to(far_row, (8, 128))
    fbuf[z] = fst[...]
    def keys_to(i, t):
        row = ROWS[i]

        @pl.when(row != z)
        def _():
            row_copies(i % NH)[1 - t].start()

        @pl.when(row == z)
        def _():
            own_copy(t, i % NH).start()

    for i, row in enumerate(ROWS):

        @pl.when(row == z)
        def _():
            own_copy(2, i % NH).start()

    for t in (1, 0):
        for i in range(6):

            @pl.when((part == i // NH) & (ROWS[i] <= z))
            def _():
                keys_to(i, t)

    for cp in loads:
        cp.wait()

    def square_sums(ref):
        f = ref[...].astype(F32)
        sq = f * f
        sq = sq[:, 0:HD] + sq[:, HD : 2 * HD] + sq[:, 2 * HD : 3 * HD]
        return jnp.sum(sq.T, axis=0, keepdims=True)

    sst[...] = jnp.concatenate(
        [square_sums(qin), square_sums(kin), jnp.zeros((6, TOK), F32)], axis=0
    )
    sbuf[y] = sst[...]

    def s_copy(yy):
        return remote(sst.at[TWO], sbuf.at[y, TWO], s_send.at[yy], s_recv.at[y], (tm, yy))

    for yy in range(ny - 1):

        @pl.when(yy < y)
        def _():
            s_copy(yy).start()

    for i in range(6):

        @pl.when((part == i // NH) & (ROWS[i] > z))
        def _():
            await_row(ROWS[i])
            keys_to(i, 1)
            keys_to(i, 0)

    for p in range(2):

        @pl.when(part == p)
        def _():
            for i in range(3 + 3 * p):
                far_to(i)

    @pl.when(part == 0)
    def _():
        for i in range(3):
            queries_to(i)

    for yy in range(1, ny):

        @pl.when(yy > y)
        def _():
            pl.semaphore_wait(hello_y.at[yy], 1)
            s_copy(yy).start()

    def arrived(ref, sem):
        remote(ref, ref, s_send.at[0], sem, dev(z, x, 1 - c)).wait_recv()

    def row_arrived(t, slot):
        ref = (v_raw.at[slot], k_raw.at[0, slot])[t]

        @pl.when(slot == slot_mine)
        def _():
            own_copy(t, 0).wait()

        @pl.when(slot != slot_mine)
        def _():
            arrived(ref, p1_recv.at[t, slot])

    def k_half(col, half):
        return k_raw.at[col, pl.ds(2 * half, 2)]

    def x_copy(t, lane, half):
        if t == 1:
            src, dst = k_half(0, half), k_half(1 + lane, half)
        else:
            src, dst = values_at[half][0].at[c], values_at[half][1 + lane].at[c]
        return remote(
            src, dst, x_send.at[t, lane, half], x_recv.at[t, lane, half],
            dev(z, lax.rem(x + (1, 3, 2)[lane], NX), c),
        )

    def x_arrived(t, lane, half):
        x_copy(t, lane, half).wait_recv()

    def c_copy(t, col, half):
        ref = (values_at, keys_at)[t][half][col].at[c]
        return remote(
            ref, ref, c_send.at[t, col, half], c_recv.at[t, col, half], dev(z, x, 1 - c)
        )

    def c_arrived(t, col, half):
        arrived((values_at, keys_at)[t][half][col].at[1 - c], c_recv.at[t, col, half])

    def spread_own(half):
        for slot in (2 * half, 2 * half + 1):
            row_arrived(1, slot)
        for ln in (2, 0, 1):
            x_copy(1, ln, half).start()
        for slot in (2 * half, 2 * half + 1):
            row_arrived(0, slot)
            values_at[half][0][c, slot - 2 * half] = v_raw[slot].reshape(2, BLK, HD)
        for ln in (2, 0, 1):
            x_copy(0, ln, half).start()
        c_copy(0, 0, half).start()

    def pass_values(half):
        for ln in (0, 1, 2):
            x_arrived(0, ln, half)
            c_copy(0, 1 + ln, half).start()

    def scaled(raw, scale, row, gain):
        scale = jnp.broadcast_to(scale[row : row + 1, :], (TOK, HD)).T
        gain = gain[pl.ds(pl.multiple_of(head * HD, HD), HD)].reshape(1, HD)
        return (raw.astype(F32) * scale * gain).astype(BF16)

    def own_scales(half):
        for i in range(2):
            slot = 2 * half + i

            @pl.when(slot != slot_mine)
            def _():
                arrived(inv_own.at[4 * part + slot, TWO], io_recv.at[4 * part + slot])

    def other_scales():
        for i in range(4):
            arrived(inv_own.at[4 - 4 * part + i, TWO], io_recv.at[4 - 4 * part + i])

    def norm_keys(col, half):
        if col > 0:
            x_arrived(1, col - 1, half)
        for i in range(2):
            slot = 2 * half + i
            if col == 0:
                scale = inv_own[4 * part + slot]
            else:
                arrived(inv_buf.at[col - 1, slot, TWO], i_recv.at[col - 1, slot])
                scale = inv_buf[col - 1, slot]
            keys = scaled(k_raw[col, slot], scale, 1, kg_in)
            keys_at[half][col][c, i] = keys.reshape(2, BLK, HD)
        c_copy(1, col, half).start()

    def norm_query(zz):
        @pl.when(zz != z)
        def _():
            arrived(q_raw.at[zz], q_recv.at[zz])

        @pl.when(zz == z)
        def _():
            own_copy(2, 0).wait()

        qbuf[zz] = scaled(q_raw[zz], inv_own[zz], 0, qg_in)

    @pl.when(active)
    def _():
        spread_own(0)
        spread_own(1)

    @pl.when(part == 1)
    def _():
        for i in range(6):
            queries_to(i)

    @pl.when(part == 0)
    def _():
        for i in range(3, 6):
            await_row(ROWS[i])
            far_to(i)
            queries_to(i)

    for yy in range(ny):

        @pl.when(yy != y)
        def _():
            arrived(sbuf.at[yy, TWO], s_recv.at[yy])

    for cp in late_loads:
        cp.wait()
    totals = sbuf[0]
    for i in range(1, ny):
        totals = totals + sbuf[i]
    inv = lax.rsqrt(totals / (NH * HD * ny) + EPS)

    isc[...] = inv

    def inv_copy(h, d):
        col = (None, 0, 2, 1)[d]
        return remote(
            isc.at[TWO], inv_buf.at[col, slot_mine, TWO], i_send.at[h, d], i_recv.at[col, slot_mine],
            dev(h + 4 * part, lax.rem(x + d, NX), c),
        )

    def io_copy(i):
        return remote(
            isc.at[TWO], inv_own.at[z, TWO], io_send.at[i], io_recv.at[z], dev(ROWS[i], x, c)
        )

    inv_own[z] = inv
    for i, row in enumerate(ROWS):

        @pl.when((row != z) & (part == i // NH))
        def _():
            io_copy(i).start()

    for h in range(NH):
        for d in (2, 1, 3):
            inv_copy(h, d).start()
    for i, row in enumerate(ROWS):

        @pl.when((row != z) & (part != i // NH))
        def _():
            io_copy(i).start()

    lane = lax.broadcasted_iota(jnp.int32, (1, HD), 1)
    lane_sq = lax.broadcasted_iota(jnp.int32, (TOK, HD), 1)

    def o_copy(zz):
        return remote(
            ost.at[zz], obuf.at[head, part], o_send.at[zz], o_recv.at[head, part], dev(zz, x, c)
        )

    def t_copy(zz):
        return remote(
            stst.at[zz, TWO], stb.at[head, part, TWO], t_send.at[zz], t_recv.at[head, part], dev(zz, x, c)
        )

    def band_slot(zz, d):
        j = zz * 8 + x * 2 + c + d
        zj = jnp.clip(j, 0, 63) // 8
        ok = (zj // 4 == part) & (j >= 0) & (j <= 63)
        return lax.rem(zj, 4), jnp.where(ok, 0.0, MASKED).astype(F32)

    def second(of, col, core, slot):
        at = lax.rem(slot, 2)
        return jnp.where(slot < 2, of[0][col][core, at, 1], of[1][col][core, at, 1])

    def attend(half, pair, zz, band):
        key_parts, value_parts = [], []
        for col in (2 * pair, 2 * pair + 1):
            for core in range(NC):
                for i in range(2):
                    owner = (4 * part + 2 * half + i) * 8 + colx[col] * 2 + core
                    pick = jnp.maximum(fsm[zz, 0, owner], 0)
                    key_parts.append(keys_at[half][col][core, i, pick])
                    value_parts.append(values_at[half][col][core, i, pick])
        add = [bias[2 * half + pair, pl.ds(zz, 1), :]]
        if band:
            slot, own = band_slot(zz, 0)
            slot_two, two = band_slot(zz, 1 - 2 * c)
            slot_three, three = band_slot(zz, 2 * c - 1)
            for of, parts in ((keys_at, key_parts), (values_at, value_parts)):
                parts.append(second(of, 0, c, slot))
                parts.append(second(of, 0, 1 - c, slot_two))
                last = jnp.where(c == 0, second(of, 1, 1, slot_three), second(of, 2, 0, slot_three))
                parts += [last, last]
            add.append(jnp.where(lane < BLK, own, two))
            add.append(jnp.where(lane < BLK, three, MASKED))
        keys = jnp.concatenate(key_parts, axis=0)
        values = jnp.concatenate(value_parts, axis=0)
        scores = lax.dot_general(
            qbuf[zz], keys, (((1,), (1,)), ((), ())), preferred_element_type=F32
        ) + jnp.concatenate(add, axis=1)
        return [scores[:, i * HD : (i + 1) * HD] for i in range(scores.shape[1] // HD)], values

    def chunk(half, pair, group):
        first, last = (half, pair) == (0, 0), (half, pair) == (1, 1)
        blocks = [group * GROUP + i for i in range(GROUP)]
        scored = [attend(half, pair, zz, last) for zz in blocks]
        tops, fades, totals_of, contexts = [], [], [], []
        for zz, (tiles, _) in zip(blocks, scored):
            top = functools.reduce(jnp.maximum, tiles)
            top = jnp.broadcast_to(jnp.max(top, axis=1, keepdims=True), (TOK, HD))
            if not first:
                old = m_ref[zz]
                top = jnp.maximum(old, top)
                fades.append(jnp.exp2((old - top) * COEF))
            tops.append(top)
        for i, (zz, (tiles, values)) in enumerate(zip(blocks, scored)):
            tiles = [jnp.exp2((t - tops[i]) * COEF) for t in tiles]
            total = functools.reduce(jnp.add, tiles)
            weights = jnp.concatenate([t.astype(BF16) for t in tiles], axis=1)
            context = jnp.dot(weights, values, preferred_element_type=F32)
            if not first:
                total = l_ref[zz] * fades[i] + total
                context = acc_ref[zz] * fades[i] + context
            totals_of.append(total)
            contexts.append(context)
        if not last:
            for zz, top, total, context in zip(blocks, tops, totals_of, contexts):
                m_ref[zz] = top
                l_ref[zz] = total
                acc_ref[zz] = context
            return
        results = []
        for top, total, context in zip(tops, totals_of, contexts):
            total = jnp.broadcast_to(jnp.sum(total, axis=1, keepdims=True), (TOK, HD))
            stats = jnp.where(lane_sq == 0, top, total).T[0:8]
            results.append(((context / total).astype(BF16), stats))
        for zz, (context, stats) in zip(blocks, results):
            ost[zz] = context
            stst[zz] = stats
        for zz, (context, stats) in zip(blocks, results):

            @pl.when(zz == z)
            def _():
                obuf[head, part] = context
                stb[head, part] = stats

            @pl.when(zz != z)
            def _():
                o_copy(zz).start()
                t_copy(zz).start()

    def far_arrived(zz):
        @pl.when(zz != z)
        def _():
            arrived(fbuf.at[zz], f_recv.at[zz])

    @pl.when(active)
    def _():
        pass_values(0)

        for zz in range(NZ):
            far_arrived(zz)
        cp = pltpu.make_async_copy(fbuf, fsm, fsm_sem)
        cp.start()
        far = fbuf[:, 0, 0:64]
        block = lax.broadcasted_iota(jnp.int32, (NZ, 64), 0) * 8 + x * 2 + c
        other = lax.broadcasted_iota(jnp.int32, (NZ, 64), 1)
        valid = jnp.where((far >= 0) | (jnp.abs(block - other) <= 1), 1.0, 0.0).astype(BF16)
        at = lax.broadcasted_iota(jnp.int32, (64, 512), 1) // BLK
        src = lax.broadcasted_iota(jnp.int32, (64, 512), 0)
        for half in range(2):
            for pair in range(2):
                zsrc = 4 * part + 2 * half + lax.rem(at, 2)
                column = jnp.where(at < 4, colx[2 * pair], colx[2 * pair + 1])
                spread = (src == zsrc * 8 + column * 2 + lax.rem(at // 2, 2)).astype(F32)
                hit = jnp.dot(valid, spread.astype(BF16), preferred_element_type=F32)
                bias[2 * half + pair] = jnp.where(hit > 0.5, 0.0, MASKED)
        cp.wait()

        def groups(group, carry):
            @pl.when((group == 0) & (part == 0))
            def _():
                own_scales(0)
                own_scales(1)

            @pl.when(group != part)
            def _():
                other_scales()

            for i in range(GROUP):
                norm_query(group * GROUP + i)

            @pl.when((group == 0) & (part == 1))
            def _():
                own_scales(0)

            @pl.when(group == 0)
            def _():
                for col in range(NX):
                    norm_keys(col, 0)
                for col in range(NX):
                    c_arrived(0, col, 0)
                    c_arrived(1, col, 0)

            chunk(0, 0, group)

            @pl.when((group == 0) & (part == 1))
            def _():
                own_scales(1)

            @pl.when(group == 0)
            def _():
                for col in range(NX):
                    norm_keys(col, 1)
                pass_values(1)

            chunk(0, 1, group)

            @pl.when(group == 0)
            def _():
                for col in range(NX):
                    c_arrived(0, col, 1)
                    c_arrived(1, col, 1)

            chunk(1, 0, group)
            chunk(1, 1, group)
            return carry

        lax.fori_loop(0, NZ // GROUP, groups, 0)

    for yy in range(ny):

        @pl.when(yy != y)
        def _():
            s_copy(yy).wait_send()

    for h in range(NH):
        for d in range(1, NX):
            inv_copy(h, d).wait_send()

        @pl.when(h + 4 * part != z)
        def _():
            for cp in row_copies(h):
                cp.wait_send()

    for i, row in enumerate(ROWS):

        @pl.when(row != z)
        def _():
            f_copy(i).wait_send()
            q_copy(i).wait_send()
            io_copy(i).wait_send()

    @pl.when(active)
    def _():
        for t in range(2):
            for ln in range(3):
                for half in range(2):
                    x_copy(t, ln, half).wait_send()
            for col in range(4):
                for half in range(2):
                    c_copy(t, col, half).wait_send()

    start = tm * TOK
    frame = start // FRAME_TOK
    after = jnp.minimum(frame + 1, 5)
    steps = lax.broadcasted_iota(jnp.int32, gate_in.shape, 0)

    def gate_of(step):
        return jnp.sum(jnp.where(steps == step, gate_in[...], 0.0), axis=0, keepdims=True)

    gate_a, gate_b = gate_of(frame_ref[frame]), gate_of(frame_ref[after])
    edge = (frame + 1) * FRAME_TOK - start
    before = lax.broadcasted_iota(jnp.int32, (TOK, HD), 0) < edge
    for h in range(NH):
        for p in range(2):

            @pl.when(h + 4 * p != z)
            def _():
                arrived(obuf.at[h, p], o_recv.at[h, p])
                arrived(stb.at[h, p, TWO], t_recv.at[h, p])

        span = slice(h * HD, (h + 1) * HD)
        one, two = stb[h, 0], stb[h, 1]
        top = jnp.maximum(one[0:1], two[0:1])
        weight_one = one[1:2] * jnp.exp2((one[0:1] - top) * COEF)
        weight_two = two[1:2] * jnp.exp2((two[0:1] - top) * COEF)
        share = weight_one / (weight_one + weight_two)
        share = jnp.broadcast_to(share, (TOK, HD)).T
        context = obuf[h, 0].astype(F32) * share + obuf[h, 1].astype(F32) * (1.0 - share)
        gate = jnp.where(before, gate_a[:, span], gate_b[:, span])
        out_ref[:, span] = (context * gate).astype(BF16)

    @pl.when(active)
    def _():
        for zz in range(NZ):

            @pl.when(zz != z)
            def _():
                o_copy(zz).wait_send()
                t_copy(zz).wait_send()


def solution(mesh):
    ny = mesh.shape["head"]
    dma = pltpu.SemaphoreType.DMA
    vmem = pltpu.VMEM

    def local(query, key, value, query_gain, key_gain, gate_table, frame_step, far_blocks):
        whole = pl.BlockSpec(memory_space=pltpu.VMEM)
        hbm = pl.BlockSpec(memory_space=pltpu.HBM)
        width = NH * HD
        return pl.pallas_call(
            functools.partial(kernel, ny),
            out_shape=pltpu.VMEM((TOK, width), BF16),
            in_specs=[hbm] * 6 + [pl.BlockSpec(memory_space=pltpu.SMEM), whole],
            out_specs=whole,
            scratch_shapes=[
                vmem((TOK, width), BF16),
                vmem((TOK, width), BF16),
                vmem((width,), F32),
                vmem((width,), F32),
                vmem((50, width), F32),
                vmem((NZ, TOK, HD), BF16),
                vmem((NX, 4, TOK, HD), BF16),
                vmem((4, TOK, HD), BF16),
                vmem((8, TOK), F32),
                vmem((NZ, 8, TOK), F32),
                vmem((NX - 1, 4, 8, TOK), F32),
                vmem((NZ, TOK, HD), BF16),
                vmem((8, 128), jnp.int32),
                vmem((NZ, 8, 128), jnp.int32),
                pltpu.SMEM((NZ, 8, 128), jnp.int32),
                vmem((8, TOK), F32),
                vmem((ny, 8, TOK), F32),
                vmem((4, NZ, 512), F32),
                vmem((NZ, TOK, HD), F32),
                vmem((NZ, TOK, HD), F32),
                vmem((NZ, TOK, HD), F32),
                vmem((NZ, TOK, HD), BF16),
                vmem((NZ, 8, TOK), F32),
                vmem((NH, 2, TOK, HD), BF16),
                vmem((NH, 2, 8, TOK), F32),
                *[vmem((NC, 2, 2, BLK, HD), BF16)] * 16,
                dma((5,)), dma((3,)), dma, pltpu.SemaphoreType.REGULAR((NZ,)),
                pltpu.SemaphoreType.REGULAR((ny,)),
                dma((ny,)), dma((ny,)), dma((6,)), dma((NZ,)), dma((6,)), dma((NZ,)),
                dma((2, 3)), dma((2, 4)), dma((6,)), dma((NZ,)), dma((3, 4)), dma((3, 4)),
                dma((2, 3, 2)), dma((2, 3, 2)),
                dma((2, 4, 2)), dma((2, 4, 2)),
                dma((NZ,)), dma((NH, 2)), dma((NZ,)), dma((NH, 2)),
            ],
            compiler_params=pltpu.CompilerParams(
                collective_id=0, has_side_effects=True, vmem_limit_bytes=56 * 2**20
            ),
            name="attend",
        )(
            query, key, value, query_gain, key_gain,
            gate_table, frame_step, far_blocks,
        )

    return jax.shard_map(
        local,
        mesh=mesh,
        in_specs=(
            P("tm", "head"),
            P("tm", "head"),
            P("tm", "head"),
            P("head"),
            P("head"),
            P(None, "head"),
            P(),
            P("tm", None),
        ),
        out_specs=P("tm", "head"),
        check_vma=False,
    )
```
